768 devices in a mesh: grp: 48 (over y, z_lo), tp: 8 (over z_hi, x), role: 2 (over core).
Axes of the slice: x: 4, y: 8, z: 12 (z_hi: 2, z_lo: 6; z = z_hi * 6 + z_lo), core: 2. Of those that a mesh axis runs over, the one named last changes fastest.
Arguments:
- teacher_rows: bfloat16 [12288, 16384], P('grp', ('tp', 'role'))
- teacher_gain: float32 [16384], P(('tp', 'role')), may hold values from 0.1 to 1.9
- block_index: int32 [128, 8], replicated, may hold values from 0 to 31, all different within a row
- block_tiles: bfloat16 [128, 8, 128, 128], P(('tp', 'role')), may hold values from -0.09375 to 0.09375
- student_shard: int32 [12288, 1], P('grp'), may hold values from 0 to 47, as said below
- student_rows: bfloat16 [23040, 4096], P('grp'), as said below
- student_gain: float32 [4096], replicated, may hold values from 0.1 to 1.9
- student_weight: bfloat16 [4096, 4096], P(None, ('tp', 'role')), may hold values from -0.09375 to 0.09375
Outputs:
- weight_grad: bfloat16 [196608, 4096], P('grp', ('tp', 'role'))
The draws below stay inside these ranges and needn't reach their ends.
Inputs may be any that keep to these rules, and one draw needn't show every extreme that they name: `block_index`: the 8 column blocks named by one row block are distinct. `student_shard`: at most 10 of the 256 tokens of one grp index go to one student shard; some student shards get exactly 10 from every grp index; every shard gets at least one token from every grp index. `student_rows`: row g*480 + s*10 + j holds the student input of the j-th token, in token order, of grp index s that goes to student shard g; rows past that number of tokens are zero.
All inputs are finite; a program needn't handle non-finite values.
Results may differ from the reference program's by a relative error of at most 0.0065.
Values may be sent and summed in bfloat16 or wider, within the bound.
No kernel may reach another device: no remote copies, remote signals or barrier semaphores. Data moves between devices by JAX's collectives and lax.ppermute only.
A program may use at most 64 MiB of HBM per device.

```python
import math
import jax
import jax.numpy as jnp
from jax import lax

DT = 16384
DS = 4096
TILE = 128
NNZ = 8
TOK_DEV = 256
TOKENS = 12288
ROWBLK = 128
COLBLK = 32
CAP = 10
HOT = 6
SLOTS = 480
N_GRP = 48


def shuffle_rows(key, count, length):
    keys = jax.random.split(key, count)
    return jax.vmap(lambda k: jax.random.permutation(k, length))(keys).astype(jnp.int32)


def route_plan(key):
    global_order = jax.random.permutation(jax.random.fold_in(key, 101), N_GRP).astype(jnp.int32)
    place = jnp.argsort(global_order).astype(jnp.int32)
    local_place = jnp.argsort(shuffle_rows(jax.random.fold_in(key, 102), N_GRP, N_GRP), axis=1).astype(jnp.int32)
    score = jnp.where(place[None, :] < HOT, place[None, :], N_GRP + local_place)
    order = jnp.argsort(score, axis=1).astype(jnp.int32)
    position = jnp.argsort(order, axis=1).astype(jnp.int32)
    rest = TOK_DEV - HOT * CAP
    base = rest // (N_GRP - HOT)
    extra = rest % (N_GRP - HOT)
    steps = jnp.arange(N_GRP, dtype=jnp.int32)
    by_pos = jnp.where(steps < HOT, CAP, base + (steps - HOT < extra).astype(jnp.int32)).astype(jnp.int32)
    counts = by_pos[position]
    ends = jnp.cumsum(by_pos)
    sorted_pos = shuffle_rows(jax.random.fold_in(key, 103), N_GRP, TOK_DEV)
    bucket = jnp.sum((ends[None, None, :] <= sorted_pos[:, :, None]).astype(jnp.int32), axis=2)
    dest = jnp.take_along_axis(order, bucket, axis=1)
    return (dest, counts)


def draw_student_shard(key, part):
    dest, counts = route_plan(key)
    return dest.reshape(TOKENS, 1).astype(jnp.int32)


def draw_student_rows(key, part):
    dest, counts = route_plan(key)
    key = jax.random.fold_in(key, 7)
    first, second, third = jax.random.split(key, 3)
    shape = (N_GRP, N_GRP, CAP, DS)
    values = jax.random.normal(first, shape, jnp.float32)
    rows = jnp.exp(jax.random.uniform(second, (N_GRP, N_GRP, CAP, 1), jnp.float32, 0.0, math.log(10.0)))
    columns = jnp.exp(jax.random.uniform(third, (DS,), jnp.float32, math.log(0.3), math.log(3.0)))
    full = values * rows * columns
    live = jnp.arange(CAP, dtype=jnp.int32)[None, None, :] < counts.T[:, :, None]
    full = jnp.where(live[:, :, :, None], full, 0.0)
    return full.reshape(N_GRP * SLOTS, DS).astype(jnp.bfloat16)


def draw_teacher_rows(key, part):
    key = jax.random.fold_in(key, 11)
    first, second, third = jax.random.split(key, 3)
    where = jnp.arange(DT, dtype=jnp.float32) / DT
    values = jax.random.normal(first, (TOKENS, DT), jnp.float32)
    rows = jnp.exp(jax.random.uniform(second, (TOKENS, 1), jnp.float32, 0.0, math.log(10.0)))
    ramp = jnp.exp(0.5 * math.log(3.0) * where)
    columns = jnp.exp(jax.random.uniform(third, (DT,), jnp.float32, 0.0, math.log(3.16))) * ramp
    return (values * rows * columns).astype(jnp.bfloat16)


def block_levels(own_key, extent, cuts, least, high):
    factor_of = 1.0
    for dim, blocks in cuts:
        steps = jax.random.uniform(jax.random.fold_in(jax.random.fold_in(own_key, 6), dim), (blocks,), jnp.float32, least / len(cuts), high / len(cuts))
        factor_of = factor_of * jnp.repeat(jnp.exp(steps), extent[dim] // blocks).reshape((-1,) + (1,) * (len(extent) - 1 - dim))
    return factor_of


def different_ones(stream_key, rows, amount, top, lift):
    sequence = jax.random.permutation(jax.random.fold_in(stream_key, 1), amount)
    boost = sequence
    for power in range(3):
        boost = boost * boost // amount
    boost = boost * lift // amount
    tickets = jax.random.randint(jax.random.fold_in(stream_key, 2), (rows, amount), 0, 4096) + boost
    fixed_rows = jax.random.permutation(jax.random.fold_in(stream_key, 3), rows)[jnp.arange(amount) % rows]
    tickets = jnp.where(jnp.arange(rows)[:, None] == fixed_rows[None, :], 1 << 14, tickets)
    merit = tickets * amount + jnp.arange(amount)
    return lax.top_k(merit.astype(jnp.int32), top)[1].astype(jnp.int32)


def bell_draw(key, dims, scale, most, shards=(), held_as=jnp.bfloat16):
    entries = scale * jax.random.normal(key, dims, jnp.float32)
    if shards:
        entries = entries * block_levels(key, dims, shards, -0.22, 0.18)
    return jnp.clip(entries, -most, most).astype(held_as)


def setup_inputs(seed: int = 0) -> dict:
    streams_of = jax.random.split(jax.random.key(seed), 9)
    return {
        "teacher_rows": draw_teacher_rows(jax.random.fold_in(streams_of[8], 71), 0),
        "teacher_gain": jnp.clip(1.0 + 0.18 * jax.random.normal(streams_of[1], (DT,), jnp.float32), 0.1, 1.9),
        "block_index": different_ones(streams_of[2], ROWBLK, COLBLK, NNZ, 0),
        "block_tiles": bell_draw(streams_of[3], (ROWBLK, NNZ, TILE, TILE), (TILE * NNZ * ROWBLK // COLBLK) ** -0.5, 0.09375, ((0, 16),)),
        "student_shard": draw_student_shard(jax.random.fold_in(streams_of[8], 71), 0),
        "student_rows": draw_student_rows(jax.random.fold_in(streams_of[8], 71), 0),
        "student_gain": jnp.clip(1.0 + 0.18 * jax.random.normal(streams_of[6], (DS,), jnp.float32), 0.1, 1.9),
        "student_weight": bell_draw(streams_of[7], (DS, DS), DS ** -0.5, 0.09375, ((1, 16),)),
    }


EPS = 1e-05

def reference(teacher_rows, teacher_gain, block_index, block_tiles, student_shard, student_rows, student_gain, student_weight):
    wide = teacher_rows.astype(jnp.float32)
    inv_norm = lax.rsqrt(lax.optimization_barrier(jnp.mean(wide * wide, axis=1)) + EPS)
    gained = (teacher_rows * teacher_gain).astype(jnp.bfloat16)
    blocks = jnp.transpose(gained.reshape(TOKENS, ROWBLK, TILE), (1, 0, 2))

    def add_block(total, inputs):
        rows, tiles, columns = inputs
        products = jnp.einsum('ti,kij->tkj', rows.astype(jnp.float32), tiles.astype(jnp.float32))
        return (total.at[:, columns].add(products), None)
    start = jnp.zeros((TOKENS, COLBLK, TILE), jnp.float32)
    projected, unused = lax.scan(add_block, start, (blocks, block_tiles, block_index))
    targets = (inv_norm[:, None, None] * projected).astype(jnp.bfloat16).reshape(TOKENS, DS)
    dest = student_shard[:, 0].reshape(N_GRP, TOK_DEV)
    hits = (dest[:, :, None] == jnp.arange(N_GRP, dtype=jnp.int32)[None, None, :]).astype(jnp.int32)
    rank = lax.optimization_barrier(jnp.sum((jnp.cumsum(hits, axis=1) - hits) * hits, axis=2))
    source = jnp.arange(N_GRP, dtype=jnp.int32)[:, None]
    slot = (dest * SLOTS + source * CAP + rank).reshape(TOKENS).astype(jnp.int32)
    slot_targets = jnp.zeros((N_GRP * SLOTS, DS), jnp.bfloat16).at[slot].set(targets)
    factor = 1.0 / math.sqrt(TOK_DEV)

    def shard_grad(inputs):
        rows, wanted = inputs
        values = rows.astype(jnp.float32)
        scale = lax.rsqrt(lax.optimization_barrier(jnp.mean(values * values, axis=1)) + EPS)
        normed = (values * scale[:, None] * student_gain).astype(jnp.bfloat16)
        student_out = jnp.dot(normed, student_weight, preferred_element_type=jnp.float32)
        out_grad = ((student_out - wanted.astype(jnp.float32)) * factor).astype(jnp.bfloat16)
        return jnp.dot(normed.T, out_grad, preferred_element_type=jnp.float32).astype(jnp.bfloat16)
    grads = lax.map(shard_grad, (student_rows.reshape(N_GRP, SLOTS, DS), slot_targets.reshape(N_GRP, SLOTS, DS)))
    return grads.reshape(N_GRP * DS, DS)
```

```python
import math

import jax
import jax.numpy as jnp
from jax import lax
from jax.experimental import pallas as pl
from jax.experimental.pallas import tpu as pltpu
from jax.sharding import PartitionSpec as P

DT = 16384
DS = 4096
TILE = 128
EPS = 1e-05
F32 = jnp.float32
BF16 = jnp.bfloat16
VMEM = pl.BlockSpec(memory_space=pltpu.VMEM)
SMEM = pl.BlockSpec(memory_space=pltpu.SMEM)
TOK = 256
CAP = 10
PAD = 24
TAIL = 16


def params():
    return pltpu.CompilerParams(vmem_limit_bytes=48 * 1024 * 1024)


def pack_sums(row):
    high = row.astype(BF16).astype(F32)
    low = row - high
    return jnp.concatenate([high, low, jnp.zeros((TAIL - 4, TILE), F32)], axis=0).astype(BF16)


def read_sums(tail):
    wide = tail.astype(F32)
    return wide[0:2] + wide[2:4]


def teacher_kernel(index_ref, rows_ref, gain_ref, tiles_ref, send_ref, keep_ref, acc):
    role = lax.axis_index("role")
    base = (lax.axis_index("tp") * 2 + role) * 8
    acc[...] = jnp.zeros_like(acc)
    squares = jnp.zeros((TOK, TILE), F32)
    for b in range(8):
        lanes = slice(b * TILE, (b + 1) * TILE)
        wide = rows_ref[:, lanes].astype(F32)
        squares = squares + wide * wide
        gained = (wide * gain_ref[:, lanes]).astype(BF16)
        tiles = jnp.concatenate([tiles_ref[b, k] for k in range(8)], axis=1)
        products = jnp.dot(gained, tiles, preferred_element_type=F32)
        for k in range(8):
            c = index_ref[k, base + b]
            own = 1 - jnp.bitwise_xor((c >> 1) & 1, role)
            place = own * 16 + ((c >> 2) & 3) * 4 + (c >> 4) * 2 + (c & 1)
            acc[place] += products[:, k * TILE : (k + 1) * TILE]
    for n in range(16):
        send_ref[n * TOK : (n + 1) * TOK, :] = acc[n].astype(BF16)
        keep_ref[n] = acc[16 + n]
    sums = jnp.sum(squares, axis=1, keepdims=True)
    row = jnp.concatenate(
        [
            jnp.transpose(jnp.broadcast_to(sums[h * TILE : (h + 1) * TILE], (TILE, TILE)))[0:1]
            for h in range(2)
        ],
        axis=0,
    )
    send_ref[16 * TOK :, :] = pack_sums(row)


def chip_kernel(send_ref, keep_ref, recv_ref, out_ref):
    tail = pack_sums(read_sums(send_ref[16 * TOK :, :]) + read_sums(recv_ref[16 * TOK :, :]))
    for x in range(4):
        for n in range(4):
            m = x * 4 + n
            out_ref[x, n * TOK : (n + 1) * TOK, :] = (
                keep_ref[m] + recv_ref[m * TOK : (m + 1) * TOK, :].astype(F32)
            ).astype(BF16)
        out_ref[x, 4 * TOK :, :] = tail


def line_kernel(recv_ref, send_ref, keep_ref):
    high = lax.axis_index("tp") // 4
    own = pl.ds(pl.multiple_of(high * 2 * TOK, 2 * TOK), 2 * TOK)
    other = pl.ds(pl.multiple_of((1 - high) * 2 * TOK, 2 * TOK), 2 * TOK)
    tail = slice(4 * TOK, 4 * TOK + TAIL)

    def total(rows):
        wide = [recv_ref[x, rows, :].astype(F32) for x in range(4)]
        return (wide[0] + wide[1]) + (wide[2] + wide[3])

    send_ref[: 2 * TOK, :] = total(other).astype(BF16)
    sums = sum(read_sums(recv_ref[x, tail, :]) for x in range(4))
    send_ref[2 * TOK :, :] = pack_sums(sums)
    keep_ref[...] = total(own)


def pack_kernel(send_ref, keep_ref, recv_ref, slot_ref, out_ref):
    sums = read_sums(send_ref[2 * TOK :, :]) + read_sums(recv_ref[2 * TOK :, :])
    inv = lax.rsqrt(sums / DT + EPS)
    scale = [
        jnp.transpose(jnp.broadcast_to(inv[h : h + 1], (TILE, TILE))) for h in range(2)
    ]
    scale = jnp.concatenate(scale, axis=0)
    rows = slot_ref[0:1, :]
    wanted = lax.broadcasted_iota(jnp.int32, (out_ref.shape[0], TOK), 0)
    packed = jnp.zeros(out_ref.shape, F32)
    for j in range(2):
        part = slice(j * TOK, (j + 1) * TOK)
        targets = (scale * (keep_ref[part, :] + recv_ref[part, :].astype(F32))).astype(BF16)
        place = jnp.where(wanted == rows + j * CAP, 1.0, 0.0).astype(BF16)
        packed = packed + jnp.dot(place, targets, preferred_element_type=F32)
    out_ref[...] = packed.astype(BF16)


def student_kernel(shard_ref, rows_ref, gain_ref, weight_ref, slot_ref, out_ref, turned_ref):
    shards = 48
    dest = shard_ref[...]
    hits = jnp.where(
        lax.broadcasted_iota(jnp.int32, (shards, TOK), 0) == dest, 1.0, 0.0
    )
    earlier = jnp.where(
        lax.broadcasted_iota(jnp.int32, (TOK, TOK), 0)
        < lax.broadcasted_iota(jnp.int32, (TOK, TOK), 1),
        1.0,
        0.0,
    ).astype(BF16)
    counts = jnp.dot(hits.astype(BF16), earlier, preferred_element_type=F32)
    rank = jnp.sum(counts * hits, axis=0, keepdims=True).astype(jnp.int32)
    slot_ref[...] = jnp.broadcast_to(dest * PAD + rank, slot_ref.shape)
    step = 512
    count = rows_ref.shape[0]
    squares = jnp.zeros((count, TILE), F32)
    for n in range(DS // TILE):
        wide = rows_ref[:, n * TILE : (n + 1) * TILE].astype(F32)
        squares = squares + wide * wide
    scale = lax.rsqrt(jnp.sum(squares, axis=1, keepdims=True) / DS + EPS)
    out_ref[...] = jnp.zeros_like(out_ref)
    for n in range(DS // step):
        part = slice(n * step, (n + 1) * step)
        normed = (rows_ref[:, part].astype(F32) * scale * gain_ref[:, part]).astype(BF16)
        out_ref[...] += jnp.dot(normed, weight_ref[part, :], preferred_element_type=F32)
        turned_ref[part, :] = jnp.transpose(normed)


def grad_kernel(recv_ref, out_ref, turned_ref, grad_ref, delta):
    @pl.when(pl.program_id(0) == 0)
    def _():
        count, rows = out_ref.shape[0], recv_ref.shape[0]
        slot = lax.broadcasted_iota(jnp.int32, (count, rows), 0)
        row = lax.broadcasted_iota(jnp.int32, (count, rows), 1)
        place = slot // CAP * PAD + slot % CAP
        for j in range(2):
            lanes = slice(j * TILE, (j + 1) * TILE)
            pick = jnp.where(row == place + j * CAP, 1.0, 0.0).astype(BF16)
            wanted = jnp.dot(pick, recv_ref[...], preferred_element_type=F32)
            delta[:, lanes] = ((out_ref[:, lanes] - wanted) * (1.0 / math.sqrt(TOK))).astype(BF16)

    grad_ref[...] = jnp.dot(
        turned_ref[...], delta[...], preferred_element_type=F32
    ).astype(BF16)


def on_device(
    teacher_rows,
    teacher_gain,
    block_index,
    block_tiles,
    student_shard,
    student_rows,
    student_gain,
    student_weight,
):
    shards = lax.axis_size("grp")
    count = student_rows.shape[0]
    send, keep = pl.pallas_call(
        teacher_kernel,
        out_shape=(
            jax.ShapeDtypeStruct((16 * TOK + TAIL, TILE), BF16),
            jax.ShapeDtypeStruct((16, TOK, TILE), F32),
        ),
        in_specs=[SMEM, VMEM, VMEM, VMEM],
        out_specs=(VMEM, VMEM),
        scratch_shapes=[pltpu.VMEM((32, TOK, TILE), F32)],
        compiler_params=params(),
        cost_estimate=pl.CostEstimate(flops=540000000, bytes_accessed=6000000, transcendentals=0),
        name="teacher",
    )(block_index.T, teacher_rows, teacher_gain[None, :], block_tiles)
    recv = lax.ppermute(send, "role", [(0, 1), (1, 0)])
    student_rows, student_shard, recv = lax.optimization_barrier(
        (student_rows, student_shard, recv)
    )
    line = pl.pallas_call(
        chip_kernel,
        out_shape=jax.ShapeDtypeStruct((4, 4 * TOK + TAIL, TILE), BF16),
        in_specs=[VMEM] * 3,
        out_specs=VMEM,
        compiler_params=params(),
        cost_estimate=pl.CostEstimate(flops=1000000, bytes_accessed=4000000, transcendentals=0),
        name="chip",
    )(send, keep, recv)
    groups = [[z * 4 + x for x in range(4)] for z in range(2)]
    line = lax.all_to_all(line, "tp", 0, 0, tiled=True, axis_index_groups=groups)
    slots, student_out, turned = pl.pallas_call(
        student_kernel,
        out_shape=(
            jax.ShapeDtypeStruct((8, TOK), jnp.int32),
            jax.ShapeDtypeStruct((count, 2 * TILE), F32),
            jax.ShapeDtypeStruct((DS, count), BF16),
        ),
        in_specs=[VMEM] * 4,
        out_specs=(VMEM,) * 3,
        compiler_params=params(),
        cost_estimate=pl.CostEstimate(flops=2000000000, bytes_accessed=10000000, transcendentals=480),
        name="student",
    )(student_shard.reshape(1, TOK), student_rows, student_gain[None, :], student_weight)
    half, own = pl.pallas_call(
        line_kernel,
        out_shape=(
            jax.ShapeDtypeStruct((2 * TOK + TAIL, TILE), BF16),
            jax.ShapeDtypeStruct((2 * TOK, TILE), F32),
        ),
        in_specs=[VMEM],
        out_specs=(VMEM, VMEM),
        compiler_params=params(),
        cost_estimate=pl.CostEstimate(flops=1000000, bytes_accessed=2000000, transcendentals=0),
        name="line",
    )(line)
    far = lax.ppermute(half, "tp", [(n, (n + 4) % 8) for n in range(8)])
    packed = pl.pallas_call(
        pack_kernel,
        out_shape=jax.ShapeDtypeStruct((shards * PAD, TILE), BF16),
        in_specs=[VMEM] * 4,
        out_specs=VMEM,
        compiler_params=params(),
        cost_estimate=pl.CostEstimate(flops=150000000, bytes_accessed=1000000, transcendentals=256),
        name="pack",
    )(half, own, far, slots)
    arrived = lax.all_to_all(
        packed.reshape(shards, PAD, TILE), "grp", split_axis=0, concat_axis=0, tiled=True
    )
    block = 1024
    return pl.pallas_call(
        grad_kernel,
        grid=(DS // block,),
        out_shape=jax.ShapeDtypeStruct((DS, 2 * TILE), BF16),
        in_specs=[
            pl.BlockSpec((shards * PAD, TILE), lambda i: (0, 0)),
            pl.BlockSpec((count, 2 * TILE), lambda i: (0, 0)),
            pl.BlockSpec((block, count), lambda i: (i, 0)),
        ],
        out_specs=pl.BlockSpec((block, 2 * TILE), lambda i: (i, 0)),
        scratch_shapes=[pltpu.VMEM((count, 2 * TILE), BF16)],
        compiler_params=params(),
        cost_estimate=pl.CostEstimate(flops=1000000000, bytes_accessed=7000000, transcendentals=0),
        name="grad",
    )(arrived.reshape(shards * PAD, TILE), student_out, turned)


def solution(mesh):
    placed = (
        P("grp", ("tp", "role")),
        P(("tp", "role")),
        P(),
        P(("tp", "role"), None, None, None),
        P("grp", None),
        P("grp", None),
        P(),
        P(None, ("tp", "role")),
    )
    return jax.shard_map(
        on_device, mesh=mesh, in_specs=placed, out_specs=P("grp", ("tp", "role")), check_vma=False
    )
```

```python
import math

import jax
import jax.numpy as jnp
from jax import lax
from jax.experimental import pallas as pl
from jax.experimental.pallas import tpu as pltpu
from jax.sharding import PartitionSpec as P

DT = 16384
DS = 4096
TILE = 128
EPS = 1e-05
F32 = jnp.float32
BF16 = jnp.bfloat16
VMEM = pl.BlockSpec(memory_space=pltpu.VMEM)
HBM = pl.BlockSpec(memory_space=pltpu.HBM)
TOK = 256
CAP = 10
PAD = 22
TEACHER_MIB = 58
ROUTE_MIB = 46
STASH = 144
TAIL = 16


def params(mib=24):
    return pltpu.CompilerParams(vmem_limit_bytes=mib * 1024 * 1024)


def pack_sums(row):
    high = row.astype(BF16).astype(F32)
    low = row - high
    return jnp.concatenate([high, low, jnp.zeros((TAIL - 4, TILE), F32)], axis=0).astype(BF16)


def read_sums(tail):
    wide = tail.astype(F32)
    return wide[0:2] + wide[2:4]


def teacher_kernel(
    index_hbm, rows_hbm, gain_hbm, tiles_hbm, send_hbm, keep_hbm,
    index, rows, gain, tiles, acc, send, own_sums, sems
):
    first = [
        pltpu.make_async_copy(rows_hbm, rows, sems.at[8]),
        pltpu.make_async_copy(gain_hbm, gain, sems.at[9]),
        pltpu.make_async_copy(index_hbm, index, sems.at[10]),
    ]
    loads = [pltpu.make_async_copy(tiles_hbm.at[b], tiles.at[b], sems.at[b]) for b in range(8)]
    for copy in first + loads:
        copy.start()
    role = lax.axis_index("role")
    base = (lax.axis_index("tp") * 2 + role) * 8
    acc[...] = jnp.zeros_like(acc)
    squares = jnp.zeros((TOK, TILE), F32)
    for copy in first:
        copy.wait()
    for b in range(8):
        lanes = slice(b * TILE, (b + 1) * TILE)
        wide = rows[:, lanes].astype(F32)
        squares = squares + wide * wide
        gained = (wide * gain[:, lanes]).astype(BF16)
        loads[b].wait()
        side = jnp.concatenate([tiles[b, k] for k in range(8)], axis=1)
        products = jnp.dot(gained, side, preferred_element_type=F32)
        for k in range(8):
            c = index[k, base + b]
            own = 1 - jnp.bitwise_xor((c >> 1) & 1, role)
            place = own * 16 + ((c >> 2) & 3) * 4 + (c >> 4) * 2 + (c & 1)
            acc[place] += products[:, k * TILE : (k + 1) * TILE]
    stores = [
        pltpu.make_async_copy(acc.at[pl.ds(16, 16)], keep_hbm.at[pl.ds(0, 16)], sems.at[11])
    ]
    stores[0].start()
    sums = jnp.sum(squares, axis=1, keepdims=True) * (1.0 / DT)
    row = jnp.concatenate(
        [
            jnp.transpose(jnp.broadcast_to(sums[h * TILE : (h + 1) * TILE], (TILE, TILE)))[0:1]
            for h in range(2)
        ],
        axis=0,
    )
    own_sums[...] = jnp.concatenate([row, jnp.zeros((TAIL - 2, TILE), F32)], axis=0)
    stores.append(
        pltpu.make_async_copy(own_sums, keep_hbm.at[16, pl.ds(0, TAIL)], sems.at[16])
    )
    stores[1].start()
    send[16 * TOK :, :] = pack_sums(row)
    step = 4 * TOK
    for m in range(4):
        for n in range(4 * m, 4 * m + 4):
            send[n * TOK : (n + 1) * TOK, :] = acc[n].astype(BF16)
        here = pl.ds(m * step, step + (TAIL if m == 3 else 0))
        stores.append(pltpu.make_async_copy(send.at[here], send_hbm.at[here], sems.at[12 + m]))
        stores[-1].start()
    for copy in stores:
        copy.wait()


def chip_kernel(tail_ref, keep_ref, recv_ref, out_ref):
    tail = pack_sums(tail_ref[0:2] + read_sums(recv_ref[16 * TOK :, :]))
    for x in range(4):
        for n in range(4):
            m = x * 4 + n
            out_ref[x, n * TOK : (n + 1) * TOK, :] = (
                keep_ref[m] + recv_ref[m * TOK : (m + 1) * TOK, :].astype(F32)
            ).astype(BF16)
        out_ref[x, 4 * TOK :, :] = tail


def route_kernel(
    shard_ref, keep_hbm, place_ref, rank_ref, hits_ref, tail_ref, keep_ref, sems
):
    copies = [
        pltpu.make_async_copy(keep_hbm.at[pl.ds(0, 16)], keep_ref, sems.at[0]),
        pltpu.make_async_copy(keep_hbm.at[16, pl.ds(0, TAIL)], tail_ref, sems.at[1]),
    ]
    for copy in copies:
        copy.start()
    dest = shard_ref[...]
    hits = jnp.where(lax.broadcasted_iota(jnp.int32, hits_ref.shape, 0) == dest, 1.0, 0.0)
    hits_ref[...] = hits.astype(BF16)
    earlier = jnp.where(
        lax.broadcasted_iota(jnp.int32, (TOK, TOK), 0)
        < lax.broadcasted_iota(jnp.int32, (TOK, TOK), 1),
        1.0,
        0.0,
    ).astype(BF16)
    counts = jnp.dot(hits.astype(BF16), earlier, preferred_element_type=F32)
    rank = jnp.sum(counts * hits, axis=0, keepdims=True).astype(jnp.int32)
    rank_ref[...] = jnp.broadcast_to(rank, rank_ref.shape)
    row = lax.broadcasted_iota(jnp.int32, (place_ref.shape[0], TOK), 0)
    for j in range(2):
        wanted = dest * PAD + 2 * rank + j
        place_ref[:, j * TOK : (j + 1) * TOK] = jnp.where(row == wanted, 1.0, 0.0).astype(BF16)
    for copy in copies:
        copy.wait()


def pack_kernel(recv_ref, place_ref, rank_ref, hits_ref, out_hbm, wide, out, sems):
    tail = slice(4 * TOK, 4 * TOK + TAIL)

    def total(n):
        part = [recv_ref[x, n * TOK : (n + 1) * TOK, :].astype(F32) for x in range(4)]
        return ((part[0] + part[1]) + (part[2] + part[3])).astype(BF16)

    sums = sum(read_sums(recv_ref[x, tail, :]) for x in range(4))
    sums = jnp.concatenate([sums[0:1], sums[1:2]], axis=1)
    high = sums.astype(BF16).astype(F32)
    slot = lax.broadcasted_iota(jnp.int32, (TILE, TOK), 0) == rank_ref[0:1, :]
    rows = place_ref.shape[0]
    parts = jnp.concatenate(
        [jnp.concatenate([total(z * 2 + j) for z in range(2)], axis=1) for j in range(2)], axis=0
    )
    moved = jnp.dot(place_ref[...], parts, preferred_element_type=F32)
    for z in range(2):
        wide[z * rows : (z + 1) * rows, :] = moved[:, z * TILE : (z + 1) * TILE]
    for n, values in enumerate((high, sums - high)):
        held = jnp.where(slot, values, 0.0).astype(BF16)
        shown = lax.dot_general(
            hits_ref[...], held, (((1,), (1,)), ((), ())), preferred_element_type=F32
        )
        for z in range(2):
            wide[pl.ds(z * rows + 2 * CAP + n, shown.shape[0], stride=PAD), :] = shown
    copies = []
    for z in range(2):
        here = pl.ds(z * rows, rows)
        out[here, :] = wide[here, :].astype(BF16)
        copies.append(pltpu.make_async_copy(out.at[here], out_hbm.at[here], sems.at[z]))
        copies[z].start()
    for copy in copies:
        copy.wait()


def student_kernel(
    rows_ref, gain_ref, weight_ref, out_ref, stash_hbm, pick_ref, spread_ref, turned_ref, sems
):
    step = DS // 8
    count = rows_ref.shape[0]
    slots = PAD // 2
    squares = jnp.zeros((count, TILE), F32)
    for n in range(DS // TILE):
        wide = rows_ref[:, n * TILE : (n + 1) * TILE].astype(F32)
        squares = squares + wide * wide
    scale = lax.rsqrt(jnp.sum(squares, axis=1, keepdims=True) / DS + EPS)
    out_ref[...] = jnp.zeros_like(out_ref)
    copies = []
    for n in range(DS // step):
        part = slice(n * step, (n + 1) * step)
        normed = (rows_ref[:, part].astype(F32) * scale * gain_ref[:, part]).astype(BF16)
        out_ref[...] += jnp.dot(normed, weight_ref[part, :], preferred_element_type=F32)
        turned_ref[part, :] = jnp.transpose(normed)
        here = pl.ds(n * step, step)
        copies.append(
            pltpu.make_async_copy(turned_ref.at[here], stash_hbm.at[here], sems.at[n])
        )
        copies[n].start()
    wanted = lax.broadcasted_iota(jnp.int32, (count, 1), 0)
    wanted = wanted + wanted // CAP
    pick_ref[...] = jnp.where(
        lax.broadcasted_iota(jnp.int32, pick_ref.shape, 1) == wanted, 1.0, 0.0
    ).astype(BF16)
    source = lax.broadcasted_iota(jnp.int32, (spread_ref.shape[0], 1), 0) // slots
    spread_ref[...] = jnp.where(
        lax.broadcasted_iota(jnp.int32, spread_ref.shape, 1) == source, 1.0, 0.0
    ).astype(BF16)
    for copy in copies:
        copy.wait()


def grad_kernel(
    recv_ref, out_ref, pick_ref, spread_ref, stash_hbm, grad_hbm, wide, turned, grad, sems
):
    steps = sems.shape[1]
    block = DS // steps
    here = [pl.ds(n * block, block) for n in range(steps)]
    loads = [
        pltpu.make_async_copy(stash_hbm.at[here[n]], turned.at[here[n]], sems.at[0, n])
        for n in range(steps)
    ]
    stores = [
        pltpu.make_async_copy(grad.at[here[n]], grad_hbm.at[here[n]], sems.at[1, n])
        for n in range(steps)
    ]
    for copy in loads:
        copy.start()
    slots = PAD // 2
    half = wide.shape[0] // 2
    count = half // 2
    shards = half // PAD
    wide[...] = recv_ref[...].astype(F32)

    def every(start, size, stride):
        return sum(wide[pl.ds(z * half + start, size, stride=stride), :] for z in range(2))

    sums = every(2 * CAP, shards, PAD) + every(2 * CAP + 1, shards, PAD)
    inv = lax.rsqrt(sums + EPS)
    high = inv.astype(BF16)
    low = (inv - high.astype(F32)).astype(BF16)
    rows = jnp.dot(
        spread_ref[...], jnp.concatenate([high, low], axis=1), preferred_element_type=F32
    )
    slot = lax.broadcasted_iota(jnp.int32, (count, 1), 0) % slots
    own = lax.broadcasted_iota(jnp.int32, (count, TILE), 1) == slot
    scale = jnp.sum(jnp.where(own, rows[:, :TILE] + rows[:, TILE:], 0.0), axis=1, keepdims=True)
    targets = jnp.concatenate(
        [(scale * every(j, count, 2)).astype(BF16) for j in range(2)], axis=1
    )
    wanted = jnp.dot(pick_ref[...], targets, preferred_element_type=F32)
    delta = ((out_ref[...] - wanted) * (1.0 / math.sqrt(TOK))).astype(BF16)
    for n in range(steps):
        loads[n].wait()
        grad[here[n], :] = jnp.dot(
            turned[here[n], :], delta, preferred_element_type=F32
        ).astype(BF16)
        stores[n].start()
    for copy in stores:
        copy.wait()


def on_device(
    teacher_rows,
    teacher_gain,
    block_index,
    block_tiles,
    student_shard,
    student_rows,
    student_gain,
    student_weight,
):
    shards = lax.axis_size("grp")
    count = student_rows.shape[0]
    send, keep = pl.pallas_call(
        teacher_kernel,
        out_shape=(
            jax.ShapeDtypeStruct((16 * TOK + TAIL, TILE), BF16),
            jax.ShapeDtypeStruct((STASH, TOK, TILE), F32),
        ),
        in_specs=[HBM] * 4,
        out_specs=(HBM, HBM),
        scratch_shapes=[
            pltpu.SMEM((8, TILE), jnp.int32),
            pltpu.VMEM(teacher_rows.shape, BF16),
            pltpu.VMEM((1, teacher_rows.shape[1]), F32),
            pltpu.VMEM(block_tiles.shape, BF16),
            pltpu.VMEM((32, TOK, TILE), F32),
            pltpu.VMEM((16 * TOK + TAIL, TILE), BF16),
            pltpu.VMEM((TAIL, TILE), F32),
            pltpu.SemaphoreType.DMA((17,)),
        ],
        compiler_params=params(TEACHER_MIB),
        cost_estimate=pl.CostEstimate(flops=540000000, bytes_accessed=6000000, transcendentals=0),
        name="teacher",
    )(block_index.T, teacher_rows, teacher_gain[None, :], block_tiles)
    recv = lax.ppermute(send, "role", [(0, 1), (1, 0)])
    student_shard, keep = lax.optimization_barrier((student_shard, keep))
    place, rank, hits, tail, keep = pl.pallas_call(
        route_kernel,
        out_shape=(
            jax.ShapeDtypeStruct((shards * PAD, 2 * TOK), BF16),
            jax.ShapeDtypeStruct((8, TOK), jnp.int32),
            jax.ShapeDtypeStruct((shards, TOK), BF16),
            jax.ShapeDtypeStruct((TAIL, TILE), F32),
            jax.ShapeDtypeStruct((16, TOK, TILE), F32),
        ),
        in_specs=[VMEM, HBM],
        out_specs=(VMEM,) * 5,
        scratch_shapes=[pltpu.SemaphoreType.DMA((2,))],
        compiler_params=params(ROUTE_MIB),
        cost_estimate=pl.CostEstimate(flops=100000000, bytes_accessed=4000000, transcendentals=0),
        name="route",
    )(student_shard.reshape(1, TOK), keep)
    place, rank, hits, tail, keep, recv = lax.optimization_barrier(
        (place, rank, hits, tail, keep, recv)
    )
    line = pl.pallas_call(
        chip_kernel,
        out_shape=jax.ShapeDtypeStruct((4, 4 * TOK + TAIL, TILE), BF16),
        in_specs=[VMEM] * 3,
        out_specs=VMEM,
        compiler_params=params(),
        cost_estimate=pl.CostEstimate(flops=1000000, bytes_accessed=4000000, transcendentals=0),
        name="chip",
    )(tail, keep, recv)
    groups = [[z * 4 + x for x in range(4)] for z in range(2)]
    line = lax.all_to_all(line, "tp", 0, 0, tiled=True, axis_index_groups=groups)
    packed = pl.pallas_call(
        pack_kernel,
        out_shape=jax.ShapeDtypeStruct((2 * shards * PAD, TILE), BF16),
        in_specs=[VMEM] * 4,
        out_specs=HBM,
        scratch_shapes=[
            pltpu.VMEM((2 * shards * PAD, TILE), F32),
            pltpu.VMEM((2 * shards * PAD, TILE), BF16),
            pltpu.SemaphoreType.DMA((2,)),
        ],
        compiler_params=params(),
        cost_estimate=pl.CostEstimate(flops=400000000, bytes_accessed=2000000, transcendentals=0),
        name="pack",
    )(line, place, rank, hits)
    student_rows, packed = lax.optimization_barrier((student_rows, packed))
    student_out, stash, pick, spread = pl.pallas_call(
        student_kernel,
        out_shape=(
            jax.ShapeDtypeStruct((count, 2 * TILE), F32),
            jax.ShapeDtypeStruct((4 * DS, count), BF16),
            jax.ShapeDtypeStruct((count, shards * PAD // 2), BF16),
            jax.ShapeDtypeStruct((shards * PAD // 2, shards), BF16),
        ),
        in_specs=[VMEM] * 3,
        out_specs=(VMEM, HBM, VMEM, VMEM),
        scratch_shapes=[pltpu.VMEM((DS, count), BF16), pltpu.SemaphoreType.DMA((8,))],
        compiler_params=params(52),
        cost_estimate=pl.CostEstimate(flops=2000000000, bytes_accessed=10000000, transcendentals=480),
        name="student",
    )(student_rows, student_gain[None, :], student_weight)
    groups = [
        [(g * 8 + z * 4 + x) * 2 + c for z in range(2) for g in range(shards)]
        for x in range(4)
        for c in range(2)
    ]
    arrived = lax.all_to_all(
        packed.reshape(2 * shards, PAD // 2, 2, TILE),
        ("grp", "tp", "role"),
        split_axis=0,
        concat_axis=0,
        tiled=True,
        axis_index_groups=groups,
    )
    rows = shards * PAD
    return pl.pallas_call(
        grad_kernel,
        out_shape=jax.ShapeDtypeStruct((DS, 2 * TILE), BF16),
        in_specs=[VMEM] * 4 + [HBM],
        out_specs=HBM,
        scratch_shapes=[
            pltpu.VMEM((2 * rows, TILE), F32),
            pltpu.VMEM((DS, count), BF16),
            pltpu.VMEM((DS, 2 * TILE), BF16),
            pltpu.SemaphoreType.DMA((2, 8)),
        ],
        compiler_params=params(52),
        cost_estimate=pl.CostEstimate(flops=1000000000, bytes_accessed=7000000, transcendentals=0),
        name="grad",
    )(arrived.reshape(2 * rows, TILE), student_out, pick, spread, stash)


def solution(mesh):
    placed = (
        P("grp", ("tp", "role")),
        P(("tp", "role")),
        P(),
        P(("tp", "role"), None, None, None),
        P("grp", None),
        P("grp", None),
        P(),
        P(None, ("tp", "role")),
    )
    return jax.shard_map(
        on_device, mesh=mesh, in_specs=placed, out_specs=P("grp", ("tp", "role")), check_vma=False
    )
```

```python
import math

import jax
import jax.numpy as jnp
from jax import lax
from jax.experimental import pallas as pl
from jax.experimental.pallas import tpu as pltpu
from jax.sharding import PartitionSpec as P

DT = 16384
DS = 4096
TILE = 128
EPS = 1e-05
F32 = jnp.float32
BF16 = jnp.bfloat16
VMEM = pl.BlockSpec(memory_space=pltpu.VMEM)
HBM = pl.BlockSpec(memory_space=pltpu.HBM)
TOK = 256
CAP = 10
PAD = 22
TEACHER_MIB = 58
ROUTE_MIB = 46
STASH = 144
TAIL = 16


def params(mib=24):
    return pltpu.CompilerParams(vmem_limit_bytes=mib * 1024 * 1024)


def pack_sums(row):
    high = row.astype(BF16).astype(F32)
    low = row - high
    return jnp.concatenate([high, low, jnp.zeros((TAIL - 4, TILE), F32)], axis=0).astype(BF16)


def read_sums(tail):
    wide = tail.astype(F32)
    return wide[0:2] + wide[2:4]


def teacher_kernel(
    index_hbm, rows_hbm, gain_hbm, tiles_hbm, send_hbm, keep_hbm,
    index, rows, gain, tiles, acc, send, own_sums, sems
):
    first = [
        pltpu.make_async_copy(rows_hbm, rows, sems.at[8]),
        pltpu.make_async_copy(gain_hbm, gain, sems.at[9]),
        pltpu.make_async_copy(index_hbm, index, sems.at[10]),
    ]
    halves = [pl.ds(0, 4), pl.ds(4, 4)]
    loads = [
        pltpu.make_async_copy(tiles_hbm.at[part], tiles.at[part], sems.at[n])
        for n, part in enumerate(halves)
    ]
    for copy in first + loads:
        copy.start()
    role = lax.axis_index("role")
    base = (lax.axis_index("tp") * 2 + role) * 8
    acc[...] = jnp.zeros_like(acc)
    squares = jnp.zeros((TOK, TILE), F32)
    for copy in first:
        copy.wait()
    for b in range(8):
        lanes = slice(b * TILE, (b + 1) * TILE)
        wide = rows[:, lanes].astype(F32)
        squares = squares + wide * wide
        gained = (wide * gain[:, lanes]).astype(BF16)
        if b % 4 == 0:
            loads[b // 4].wait()
        side = jnp.concatenate([tiles[b, k] for k in range(8)], axis=1)
        products = jnp.dot(gained, side, preferred_element_type=F32)
        for k in range(8):
            c = index[k, base + b]
            own = 1 - jnp.bitwise_xor((c >> 1) & 1, role)
            place = own * 16 + ((c >> 2) & 3) * 4 + (c >> 4) * 2 + (c & 1)
            acc[place] += products[:, k * TILE : (k + 1) * TILE]
    stores = [
        pltpu.make_async_copy(acc.at[pl.ds(16, 16)], keep_hbm.at[pl.ds(0, 16)], sems.at[11])
    ]
    stores[0].start()
    sums = jnp.sum(squares, axis=1, keepdims=True) * (1.0 / DT)
    row = jnp.concatenate(
        [
            jnp.transpose(jnp.broadcast_to(sums[h * TILE : (h + 1) * TILE], (TILE, TILE)))[0:1]
            for h in range(2)
        ],
        axis=0,
    )
    own_sums[...] = jnp.concatenate([row, jnp.zeros((TAIL - 2, TILE), F32)], axis=0)
    stores.append(
        pltpu.make_async_copy(own_sums, keep_hbm.at[16, pl.ds(0, TAIL)], sems.at[16])
    )
    stores[1].start()
    send[16 * TOK :, :] = pack_sums(row)
    step = 4 * TOK
    for m in range(4):
        for n in range(4 * m, 4 * m + 4):
            send[n * TOK : (n + 1) * TOK, :] = acc[n].astype(BF16)
        here = pl.ds(m * step, step + (TAIL if m == 3 else 0))
        stores.append(pltpu.make_async_copy(send.at[here], send_hbm.at[here], sems.at[12 + m]))
        stores[-1].start()
    for copy in stores:
        copy.wait()


def chip_kernel(tail_ref, keep_ref, recv_ref, out_ref):
    tail = pack_sums(tail_ref[0:2] + read_sums(recv_ref[16 * TOK :, :]))
    for x in range(4):
        for n in range(4):
            m = x * 4 + n
            out_ref[x, n * TOK : (n + 1) * TOK, :] = (
                keep_ref[m] + recv_ref[m * TOK : (m + 1) * TOK, :].astype(F32)
            ).astype(BF16)
        out_ref[x, 4 * TOK :, :] = tail


def route_kernel(
    shard_ref, keep_hbm, place_ref, rank_ref, hits_ref, tail_ref, keep_ref, sems
):
    copies = [
        pltpu.make_async_copy(keep_hbm.at[pl.ds(0, 16)], keep_ref, sems.at[0]),
        pltpu.make_async_copy(keep_hbm.at[16, pl.ds(0, TAIL)], tail_ref, sems.at[1]),
    ]
    for copy in copies:
        copy.start()
    dest = shard_ref[...]
    hits = jnp.where(lax.broadcasted_iota(jnp.int32, hits_ref.shape, 0) == dest, 1.0, 0.0)
    hits_ref[...] = hits.astype(BF16)
    earlier = jnp.where(
        lax.broadcasted_iota(jnp.int32, (TOK, TOK), 0)
        < lax.broadcasted_iota(jnp.int32, (TOK, TOK), 1),
        1.0,
        0.0,
    ).astype(BF16)
    counts = jnp.dot(hits.astype(BF16), earlier, preferred_element_type=F32)
    rank = jnp.sum(counts * hits, axis=0, keepdims=True).astype(jnp.int32)
    rank_ref[...] = jnp.broadcast_to(rank, rank_ref.shape)
    row = lax.broadcasted_iota(jnp.int32, (place_ref.shape[0], TOK), 0)
    for j in range(2):
        wanted = dest * PAD + 2 * rank + j
        place_ref[:, j * TOK : (j + 1) * TOK] = jnp.where(row == wanted, 1.0, 0.0).astype(BF16)
    for copy in copies:
        copy.wait()


def pack_kernel(recv_ref, place_ref, rank_ref, hits_ref, out_hbm, wide, out, sems):
    tail = slice(4 * TOK, 4 * TOK + TAIL)

    def total(n):
        part = [recv_ref[x, n * TOK : (n + 1) * TOK, :].astype(F32) for x in range(4)]
        return ((part[0] + part[1]) + (part[2] + part[3])).astype(BF16)

    sums = sum(read_sums(recv_ref[x, tail, :]) for x in range(4))
    sums = jnp.concatenate([sums[0:1], sums[1:2]], axis=1)
    high = sums.astype(BF16).astype(F32)
    slot = lax.broadcasted_iota(jnp.int32, (TILE, TOK), 0) == rank_ref[0:1, :]
    rows = place_ref.shape[0]
    parts = jnp.concatenate(
        [jnp.concatenate([total(z * 2 + j) for z in range(2)], axis=1) for j in range(2)], axis=0
    )
    moved = jnp.dot(place_ref[...], parts, preferred_element_type=F32)
    for z in range(2):
        wide[z * rows : (z + 1) * rows, :] = moved[:, z * TILE : (z + 1) * TILE]
    for n, values in enumerate((high, sums - high)):
        held = jnp.where(slot, values, 0.0).astype(BF16)
        shown = lax.dot_general(
            hits_ref[...], held, (((1,), (1,)), ((), ())), preferred_element_type=F32
        )
        for z in range(2):
            wide[pl.ds(z * rows + 2 * CAP + n, shown.shape[0], stride=PAD), :] = shown
    copies = []
    for z in range(2):
        here = pl.ds(z * rows, rows)
        out[here, :] = wide[here, :].astype(BF16)
        copies.append(pltpu.make_async_copy(out.at[here], out_hbm.at[here], sems.at[z]))
        copies[z].start()
    for copy in copies:
        copy.wait()


def student_kernel(
    rows_ref, gain_ref, weight_ref, out_ref, stash_hbm, spread_ref, own_ref, turned_ref, sems
):
    step = DS // 8
    count = rows_ref.shape[0]
    slots = PAD // 2
    squares = jnp.zeros((count, TILE), F32)
    for n in range(DS // TILE):
        wide = rows_ref[:, n * TILE : (n + 1) * TILE].astype(F32)
        squares = squares + wide * wide
    scale = lax.rsqrt(jnp.sum(squares, axis=1, keepdims=True) / DS + EPS)
    out_ref[...] = jnp.zeros_like(out_ref)
    copies = []
    for n in range(DS // step):
        part = slice(n * step, (n + 1) * step)
        normed = (rows_ref[:, part].astype(F32) * scale * gain_ref[:, part]).astype(BF16)
        out_ref[...] += jnp.dot(normed, weight_ref[part, :], preferred_element_type=F32)
        turned_ref[part, :] = jnp.transpose(normed)
        here = pl.ds(n * step, step)
        copies.append(
            pltpu.make_async_copy(turned_ref.at[here], stash_hbm.at[here], sems.at[n])
        )
        copies[n].start()
    row = lax.broadcasted_iota(jnp.int32, (spread_ref.shape[0], 1), 0)
    source = row // slots
    own_ref[...] = jnp.where(
        lax.broadcasted_iota(jnp.int32, own_ref.shape, 1) == row - source * slots, 1.0, 0.0
    )
    spread_ref[...] = jnp.where(
        lax.broadcasted_iota(jnp.int32, spread_ref.shape, 1) == source, 1.0, 0.0
    ).astype(BF16)
    for copy in copies:
        copy.wait()


def grad_kernel(
    recv_ref, out_ref, spread_ref, own_ref, stash_hbm, grad_hbm, wide, turned, grad, sems
):
    steps = sems.shape[1]
    block = DS // steps
    here = [pl.ds(n * block, block) for n in range(steps)]
    loads = {
        n: pltpu.make_async_copy(
            stash_hbm.at[pl.ds(n * block, size * block)],
            turned.at[pl.ds(n * block, size * block)],
            sems.at[0, n],
        )
        for n, size in ((0, 1), (1, 3), (4, 4))
    }
    stores = [
        pltpu.make_async_copy(grad.at[here[n]], grad_hbm.at[here[n]], sems.at[1, n])
        for n in range(steps)
    ]
    for copy in loads.values():
        copy.start()
    half = wide.shape[0] // 2
    count = half // 2
    shards = half // PAD
    row = lax.broadcasted_iota(jnp.int32, (1, count), 1)
    source = row // (PAD // 2)
    row = jnp.where(row - source * (PAD // 2) < CAP, row - source, -1)
    pick = jnp.where(
        lax.broadcasted_iota(jnp.int32, (out_ref.shape[0], count), 0) == row, 1.0, 0.0
    ).astype(BF16)
    wide[...] = recv_ref[...].astype(F32)

    def every(start, size, stride):
        return sum(wide[pl.ds(z * half + start, size, stride=stride), :] for z in range(2))

    sums = every(2 * CAP, shards, PAD) + every(2 * CAP + 1, shards, PAD)
    inv = lax.rsqrt(sums + EPS)
    high = inv.astype(BF16)
    low = (inv - high.astype(F32)).astype(BF16)
    rows = jnp.dot(
        spread_ref[...], jnp.concatenate([high, low], axis=1), preferred_element_type=F32
    )
    scale = jnp.sum(own_ref[...] * (rows[:, :TILE] + rows[:, TILE:]), axis=1, keepdims=True)
    targets = jnp.concatenate(
        [(scale * every(j, count, 2)).astype(BF16) for j in range(2)], axis=1
    )
    wanted = jnp.dot(pick, targets, preferred_element_type=F32)
    delta = ((out_ref[...] - wanted) * (1.0 / math.sqrt(TOK))).astype(BF16)
    for n in range(steps):
        if n in loads:
            loads[n].wait()
        grad[here[n], :] = jnp.dot(
            turned[here[n], :], delta, preferred_element_type=F32
        ).astype(BF16)
        stores[n].start()
    for copy in stores:
        copy.wait()


def on_device(
    teacher_rows,
    teacher_gain,
    block_index,
    block_tiles,
    student_shard,
    student_rows,
    student_gain,
    student_weight,
):
    shards = lax.axis_size("grp")
    count = student_rows.shape[0]
    send, keep = pl.pallas_call(
        teacher_kernel,
        out_shape=(
            jax.ShapeDtypeStruct((16 * TOK + TAIL, TILE), BF16),
            jax.ShapeDtypeStruct((STASH, TOK, TILE), F32),
        ),
        in_specs=[HBM] * 4,
        out_specs=(HBM, HBM),
        scratch_shapes=[
            pltpu.SMEM((8, TILE), jnp.int32),
            pltpu.VMEM(teacher_rows.shape, BF16),
            pltpu.VMEM((1, teacher_rows.shape[1]), F32),
            pltpu.VMEM(block_tiles.shape, BF16),
            pltpu.VMEM((32, TOK, TILE), F32),
            pltpu.VMEM((16 * TOK + TAIL, TILE), BF16),
            pltpu.VMEM((TAIL, TILE), F32),
            pltpu.SemaphoreType.DMA((17,)),
        ],
        compiler_params=params(TEACHER_MIB),
        cost_estimate=pl.CostEstimate(flops=540000000, bytes_accessed=6000000, transcendentals=0),
        name="teacher",
    )(block_index.T, teacher_rows, teacher_gain[None, :], block_tiles)
    recv = lax.ppermute(send, "role", [(0, 1), (1, 0)])
    student_shard, keep = lax.optimization_barrier((student_shard, keep))
    place, rank, hits, tail, keep = pl.pallas_call(
        route_kernel,
        out_shape=(
            jax.ShapeDtypeStruct((shards * PAD, 2 * TOK), BF16),
            jax.ShapeDtypeStruct((8, TOK), jnp.int32),
            jax.ShapeDtypeStruct((shards, TOK), BF16),
            jax.ShapeDtypeStruct((TAIL, TILE), F32),
            jax.ShapeDtypeStruct((16, TOK, TILE), F32),
        ),
        in_specs=[VMEM, HBM],
        out_specs=(VMEM,) * 5,
        scratch_shapes=[pltpu.SemaphoreType.DMA((2,))],
        compiler_params=params(ROUTE_MIB),
        cost_estimate=pl.CostEstimate(flops=100000000, bytes_accessed=4000000, transcendentals=0),
        name="route",
    )(student_shard.reshape(1, TOK), keep)
    place, rank, hits, tail, keep, recv = lax.optimization_barrier(
        (place, rank, hits, tail, keep, recv)
    )
    line = pl.pallas_call(
        chip_kernel,
        out_shape=jax.ShapeDtypeStruct((4, 4 * TOK + TAIL, TILE), BF16),
        in_specs=[VMEM] * 3,
        out_specs=VMEM,
        compiler_params=params(),
        cost_estimate=pl.CostEstimate(flops=1000000, bytes_accessed=4000000, transcendentals=0),
        name="chip",
    )(tail, keep, recv)
    groups = [[z * 4 + x for x in range(4)] for z in range(2)]
    line = lax.all_to_all(line, "tp", 0, 0, tiled=True, axis_index_groups=groups)
    packed = pl.pallas_call(
        pack_kernel,
        out_shape=jax.ShapeDtypeStruct((2 * shards * PAD, TILE), BF16),
        in_specs=[VMEM] * 4,
        out_specs=HBM,
        scratch_shapes=[
            pltpu.VMEM((2 * shards * PAD, TILE), F32),
            pltpu.VMEM((2 * shards * PAD, TILE), BF16),
            pltpu.SemaphoreType.DMA((2,)),
        ],
        compiler_params=params(),
        cost_estimate=pl.CostEstimate(flops=400000000, bytes_accessed=2000000, transcendentals=0),
        name="pack",
    )(line, place, rank, hits)
    student_rows, packed = lax.optimization_barrier((student_rows, packed))
    student_out, stash, spread, own = pl.pallas_call(
        student_kernel,
        out_shape=(
            jax.ShapeDtypeStruct((count, 2 * TILE), F32),
            jax.ShapeDtypeStruct((4 * DS, count), BF16),
            jax.ShapeDtypeStruct((shards * PAD // 2, shards), BF16),
            jax.ShapeDtypeStruct((shards * PAD // 2, TILE), F32),
        ),
        in_specs=[VMEM] * 3,
        out_specs=(VMEM, HBM, VMEM, VMEM),
        scratch_shapes=[pltpu.VMEM((DS, count), BF16), pltpu.SemaphoreType.DMA((8,))],
        compiler_params=params(52),
        cost_estimate=pl.CostEstimate(flops=2000000000, bytes_accessed=10000000, transcendentals=480),
        name="student",
    )(student_rows, student_gain[None, :], student_weight)
    groups = [
        [(g * 8 + z * 4 + x) * 2 + c for z in range(2) for g in range(shards)]
        for x in range(4)
        for c in range(2)
    ]
    arrived = lax.all_to_all(
        packed.reshape(2 * shards, PAD // 2, 2, TILE),
        ("grp", "tp", "role"),
        split_axis=0,
        concat_axis=0,
        tiled=True,
        axis_index_groups=groups,
    )
    rows = shards * PAD
    return pl.pallas_call(
        grad_kernel,
        out_shape=jax.ShapeDtypeStruct((DS, 2 * TILE), BF16),
        in_specs=[VMEM] * 4 + [HBM],
        out_specs=HBM,
        scratch_shapes=[
            pltpu.VMEM((2 * rows, TILE), F32),
            pltpu.VMEM((DS, count), BF16),
            pltpu.VMEM((DS, 2 * TILE), BF16),
            pltpu.SemaphoreType.DMA((2, 8)),
        ],
        compiler_params=params(52),
        cost_estimate=pl.CostEstimate(flops=1000000000, bytes_accessed=7000000, transcendentals=0),
        name="grad",
    )(arrived.reshape(2 * rows, TILE), student_out, spread, own, stash)


def solution(mesh):
    placed = (
        P("grp", ("tp", "role")),
        P(("tp", "role")),
        P(),
        P(("tp", "role"), None, None, None),
        P("grp", None),
        P("grp", None),
        P(),
        P(None, ("tp", "role")),
    )
    return jax.shard_map(
        on_device, mesh=mesh, in_specs=placed, out_specs=P("grp", ("tp", "role")), check_vma=False
    )
```

```python
import math

import jax
import jax.numpy as jnp
from jax import lax
from jax.experimental import pallas as pl
from jax.experimental.pallas import tpu as pltpu
from jax.sharding import PartitionSpec as P

DT = 16384
DS = 4096
TILE = 128
EPS = 1e-05
F32 = jnp.float32
BF16 = jnp.bfloat16
VMEM = pl.BlockSpec(memory_space=pltpu.VMEM)
HBM = pl.BlockSpec(memory_space=pltpu.HBM)
TOK = 256
CAP = 10
PAD = 22
TEACHER_MIB = 58
ROUTE_MIB = 46
STASH = 144
TAIL = 16


def params(mib=24):
    return pltpu.CompilerParams(vmem_limit_bytes=mib * 1024 * 1024)


def pack_sums(row):
    high = row.astype(BF16).astype(F32)
    low = row - high
    return jnp.concatenate([high, low, jnp.zeros((TAIL - 4, TILE), F32)], axis=0).astype(BF16)


def read_sums(tail):
    wide = tail.astype(F32)
    return wide[0:2] + wide[2:4]


def teacher_kernel(
    index_hbm, rows_hbm, gain_hbm, tiles_hbm, send_hbm, keep_hbm,
    index, rows, gain, tiles, acc, send, own_sums, sems
):
    first = [
        pltpu.make_async_copy(rows_hbm, rows, sems.at[8]),
        pltpu.make_async_copy(gain_hbm, gain, sems.at[9]),
        pltpu.make_async_copy(index_hbm, index, sems.at[10]),
    ]
    halves = [pl.ds(0, 4), pl.ds(4, 4)]
    loads = [
        pltpu.make_async_copy(tiles_hbm.at[part], tiles.at[part], sems.at[n])
        for n, part in enumerate(halves)
    ]
    for copy in first + loads:
        copy.start()
    role = lax.axis_index("role")
    base = (lax.axis_index("tp") * 2 + role) * 8
    acc[...] = jnp.zeros_like(acc)
    squares = jnp.zeros((TOK, TILE), F32)
    for copy in first:
        copy.wait()
    for b in range(8):
        lanes = slice(b * TILE, (b + 1) * TILE)
        wide = rows[:, lanes].astype(F32)
        squares = squares + wide * wide
        gained = (wide * gain[:, lanes]).astype(BF16)
        if b % 4 == 0:
            loads[b // 4].wait()
        side = jnp.concatenate([tiles[b, k] for k in range(8)], axis=1)
        products = jnp.dot(gained, side, preferred_element_type=F32)
        for k in range(8):
            c = index[k, base + b]
            own = 1 - jnp.bitwise_xor((c >> 1) & 1, role)
            place = own * 16 + ((c >> 2) & 3) * 4 + (c >> 4) * 2 + (c & 1)
            acc[place] += products[:, k * TILE : (k + 1) * TILE]
    stores = [
        pltpu.make_async_copy(acc.at[pl.ds(16, 16)], keep_hbm.at[pl.ds(0, 16)], sems.at[11])
    ]
    stores[0].start()
    sums = jnp.sum(squares, axis=1, keepdims=True) * (1.0 / DT)
    row = jnp.concatenate(
        [
            jnp.transpose(jnp.broadcast_to(sums[h * TILE : (h + 1) * TILE], (TILE, TILE)))[0:1]
            for h in range(2)
        ],
        axis=0,
    )
    own_sums[...] = jnp.concatenate([row, jnp.zeros((TAIL - 2, TILE), F32)], axis=0)
    stores.append(
        pltpu.make_async_copy(own_sums, keep_hbm.at[16, pl.ds(0, TAIL)], sems.at[16])
    )
    stores[1].start()
    send[16 * TOK :, :] = pack_sums(row)
    step = 4 * TOK
    for m in range(4):
        for n in range(4 * m, 4 * m + 4):
            send[n * TOK : (n + 1) * TOK, :] = acc[n].astype(BF16)
        here = pl.ds(m * step, step + (TAIL if m == 3 else 0))
        stores.append(pltpu.make_async_copy(send.at[here], send_hbm.at[here], sems.at[12 + m]))
        stores[-1].start()
    for copy in stores:
        copy.wait()


def chip_kernel(tail_ref, keep_ref, recv_ref, out_ref):
    tail = pack_sums(tail_ref[0:2] + read_sums(recv_ref[16 * TOK :, :]))
    for x in range(4):
        for n in range(4):
            m = x * 4 + n
            out_ref[x, n * TOK : (n + 1) * TOK, :] = (
                keep_ref[m] + recv_ref[m * TOK : (m + 1) * TOK, :].astype(F32)
            ).astype(BF16)
        out_ref[x, 4 * TOK :, :] = tail


def route_kernel(
    shard_ref, keep_hbm, place_ref, rank_ref, hits_ref, tail_ref, keep_ref, sems
):
    copies = [
        pltpu.make_async_copy(keep_hbm.at[pl.ds(0, 16)], keep_ref, sems.at[0]),
        pltpu.make_async_copy(keep_hbm.at[16, pl.ds(0, TAIL)], tail_ref, sems.at[1]),
    ]
    for copy in copies:
        copy.start()
    dest = shard_ref[...]
    hits = jnp.where(lax.broadcasted_iota(jnp.int32, hits_ref.shape, 0) == dest, 1.0, 0.0)
    hits_ref[...] = hits.astype(BF16)
    earlier = jnp.where(
        lax.broadcasted_iota(jnp.int32, (TOK, TOK), 0)
        < lax.broadcasted_iota(jnp.int32, (TOK, TOK), 1),
        1.0,
        0.0,
    ).astype(BF16)
    counts = jnp.dot(hits.astype(BF16), earlier, preferred_element_type=F32)
    rank = jnp.sum(counts * hits, axis=0, keepdims=True).astype(jnp.int32)
    rank_ref[...] = jnp.broadcast_to(rank, rank_ref.shape)
    row = lax.broadcasted_iota(jnp.int32, (place_ref.shape[0], TOK), 0)
    for j in range(2):
        wanted = dest * PAD + 2 * rank + j
        place_ref[:, j * TOK : (j + 1) * TOK] = jnp.where(row == wanted, 1.0, 0.0).astype(BF16)
    for copy in copies:
        copy.wait()


def pack_kernel(recv_ref, place_ref, rank_ref, hits_ref, out_hbm, wide, out, sems):
    tail = slice(4 * TOK, 4 * TOK + TAIL)

    def total(n):
        part = [recv_ref[x, n * TOK : (n + 1) * TOK, :].astype(F32) for x in range(4)]
        return ((part[0] + part[1]) + (part[2] + part[3])).astype(BF16)

    sums = sum(read_sums(recv_ref[x, tail, :]) for x in range(4))
    sums = jnp.concatenate([sums[0:1], sums[1:2]], axis=1)
    high = sums.astype(BF16).astype(F32)
    slot = lax.broadcasted_iota(jnp.int32, (TILE, TOK), 0) == rank_ref[0:1, :]
    rows = place_ref.shape[0]
    parts = jnp.concatenate(
        [jnp.concatenate([total(z * 2 + j) for z in range(2)], axis=1) for j in range(2)], axis=0
    )
    moved = jnp.dot(place_ref[...], parts, preferred_element_type=F32)
    for z in range(2):
        wide[z * rows : (z + 1) * rows, :] = moved[:, z * TILE : (z + 1) * TILE]
    for n, values in enumerate((high, sums - high)):
        held = jnp.where(slot, values, 0.0).astype(BF16)
        shown = lax.dot_general(
            hits_ref[...], held, (((1,), (1,)), ((), ())), preferred_element_type=F32
        )
        for z in range(2):
            wide[pl.ds(z * rows + 2 * CAP + n, shown.shape[0], stride=PAD), :] = shown
    copies = []
    for z in range(2):
        here = pl.ds(z * rows, rows)
        out[here, :] = wide[here, :].astype(BF16)
        copies.append(pltpu.make_async_copy(out.at[here], out_hbm.at[here], sems.at[z]))
        copies[z].start()
    for copy in copies:
        copy.wait()


def student_work(rows_hbm, gain_hbm, weight_hbm, out_ref, stash_hbm, rows, gain, weight, turned, sems):
    steps = 8
    step = DS // steps
    loads = [
        pltpu.make_async_copy(rows_hbm, rows, sems.at[steps]),
        pltpu.make_async_copy(gain_hbm, gain, sems.at[steps + 1]),
        pltpu.make_async_copy(weight_hbm, weight, sems.at[steps + 2]),
    ]
    for copy in loads:
        copy.start()
    count = rows.shape[0]
    squares = jnp.zeros((count, TILE), F32)
    loads[0].wait()
    for n in range(DS // TILE):
        wide = rows[:, n * TILE : (n + 1) * TILE].astype(F32)
        squares = squares + wide * wide
    scale = lax.rsqrt(jnp.sum(squares, axis=1, keepdims=True) / DS + EPS)
    out_ref[...] = jnp.zeros_like(out_ref)
    loads[1].wait()
    loads[2].wait()
    copies = []
    for n in range(steps):
        part = slice(n * step, (n + 1) * step)
        normed = (rows[:, part].astype(F32) * scale * gain[:, part]).astype(BF16)
        out_ref[...] += jnp.dot(normed, weight[part, :], preferred_element_type=F32)
        turned[part, :] = jnp.transpose(normed)
        here = pl.ds(n * step, step)
        copies.append(pltpu.make_async_copy(turned.at[here], stash_hbm.at[here], sems.at[n]))
        copies[n].start()
    for copy in copies:
        copy.wait()


def early_student_kernel(rows_hbm, gain_hbm, weight_hbm, line_ref, out_ref, stash_hbm, *scratch):
    @pl.when(lax.axis_index("role") == 0)
    def _():
        student_work(rows_hbm, gain_hbm, weight_hbm, out_ref, stash_hbm, *scratch)


def late_student_kernel(
    rows_hbm, gain_hbm, weight_hbm, early_ref, early_hbm, out_ref, stash_hbm, spread_ref, own_ref, *scratch
):
    @pl.when(lax.axis_index("role") == 0)
    def _():
        out_ref[...] = early_ref[...]

    @pl.when(lax.axis_index("role") == 1)
    def _():
        student_work(rows_hbm, gain_hbm, weight_hbm, out_ref, stash_hbm, *scratch)

    slots = PAD // 2
    row = lax.broadcasted_iota(jnp.int32, (spread_ref.shape[0], 1), 0)
    source = row // slots
    own_ref[...] = jnp.where(
        lax.broadcasted_iota(jnp.int32, own_ref.shape, 1) == row - source * slots, 1.0, 0.0
    )
    spread_ref[...] = jnp.where(
        lax.broadcasted_iota(jnp.int32, spread_ref.shape, 1) == source, 1.0, 0.0
    ).astype(BF16)


def grad_kernel(
    recv_ref, out_ref, spread_ref, own_ref, stash_hbm, grad_hbm, wide, turned, grad, sems
):
    steps = sems.shape[1]
    block = DS // steps
    here = [pl.ds(n * block, block) for n in range(steps)]
    loads = {
        n: pltpu.make_async_copy(
            stash_hbm.at[pl.ds(n * block, size * block)],
            turned.at[pl.ds(n * block, size * block)],
            sems.at[0, n],
        )
        for n, size in ((0, 1), (1, 3), (4, 4))
    }
    stores = [
        pltpu.make_async_copy(grad.at[here[n]], grad_hbm.at[here[n]], sems.at[1, n])
        for n in range(steps)
    ]
    for copy in loads.values():
        copy.start()
    half = wide.shape[0] // 2
    count = half // 2
    shards = half // PAD
    row = lax.broadcasted_iota(jnp.int32, (1, count), 1)
    source = row // (PAD // 2)
    row = jnp.where(row - source * (PAD // 2) < CAP, row - source, -1)
    pick = jnp.where(
        lax.broadcasted_iota(jnp.int32, (out_ref.shape[0], count), 0) == row, 1.0, 0.0
    ).astype(BF16)
    wide[...] = recv_ref[...].astype(F32)

    def every(start, size, stride):
        return sum(wide[pl.ds(z * half + start, size, stride=stride), :] for z in range(2))

    sums = every(2 * CAP, shards, PAD) + every(2 * CAP + 1, shards, PAD)
    inv = lax.rsqrt(sums + EPS)
    high = inv.astype(BF16)
    low = (inv - high.astype(F32)).astype(BF16)
    rows = jnp.dot(
        spread_ref[...], jnp.concatenate([high, low], axis=1), preferred_element_type=F32
    )
    scale = jnp.sum(own_ref[...] * (rows[:, :TILE] + rows[:, TILE:]), axis=1, keepdims=True)
    targets = jnp.concatenate(
        [(scale * every(j, count, 2)).astype(BF16) for j in range(2)], axis=1
    )
    wanted = jnp.dot(pick, targets, preferred_element_type=F32)
    delta = ((out_ref[...] - wanted) * (1.0 / math.sqrt(TOK))).astype(BF16)
    for n in range(steps):
        if n in loads:
            loads[n].wait()
        grad[here[n], :] = jnp.dot(
            turned[here[n], :], delta, preferred_element_type=F32
        ).astype(BF16)
        stores[n].start()
    for copy in stores:
        copy.wait()


def on_device(
    teacher_rows,
    teacher_gain,
    block_index,
    block_tiles,
    student_shard,
    student_rows,
    student_gain,
    student_weight,
):
    shards = lax.axis_size("grp")
    count = student_rows.shape[0]
    send, keep = pl.pallas_call(
        teacher_kernel,
        out_shape=(
            jax.ShapeDtypeStruct((16 * TOK + TAIL, TILE), BF16),
            jax.ShapeDtypeStruct((STASH, TOK, TILE), F32),
        ),
        in_specs=[HBM] * 4,
        out_specs=(HBM, HBM),
        scratch_shapes=[
            pltpu.SMEM((8, TILE), jnp.int32),
            pltpu.VMEM(teacher_rows.shape, BF16),
            pltpu.VMEM((1, teacher_rows.shape[1]), F32),
            pltpu.VMEM(block_tiles.shape, BF16),
            pltpu.VMEM((32, TOK, TILE), F32),
            pltpu.VMEM((16 * TOK + TAIL, TILE), BF16),
            pltpu.VMEM((TAIL, TILE), F32),
            pltpu.SemaphoreType.DMA((17,)),
        ],
        compiler_params=params(TEACHER_MIB),
        cost_estimate=pl.CostEstimate(flops=540000000, bytes_accessed=6000000, transcendentals=0),
        name="teacher",
    )(block_index.T, teacher_rows, teacher_gain[None, :], block_tiles)
    recv = lax.ppermute(send, "role", [(0, 1), (1, 0)])
    student_shard, keep = lax.optimization_barrier((student_shard, keep))
    place, rank, hits, tail, keep = pl.pallas_call(
        route_kernel,
        out_shape=(
            jax.ShapeDtypeStruct((shards * PAD, 2 * TOK), BF16),
            jax.ShapeDtypeStruct((8, TOK), jnp.int32),
            jax.ShapeDtypeStruct((shards, TOK), BF16),
            jax.ShapeDtypeStruct((TAIL, TILE), F32),
            jax.ShapeDtypeStruct((16, TOK, TILE), F32),
        ),
        in_specs=[VMEM, HBM],
        out_specs=(VMEM,) * 5,
        scratch_shapes=[pltpu.SemaphoreType.DMA((2,))],
        compiler_params=params(ROUTE_MIB),
        cost_estimate=pl.CostEstimate(flops=100000000, bytes_accessed=4000000, transcendentals=0),
        name="route",
    )(student_shard.reshape(1, TOK), keep)
    place, rank, hits, tail, keep, recv = lax.optimization_barrier(
        (place, rank, hits, tail, keep, recv)
    )
    line = pl.pallas_call(
        chip_kernel,
        out_shape=jax.ShapeDtypeStruct((4, 4 * TOK + TAIL, TILE), BF16),
        in_specs=[VMEM] * 3,
        out_specs=VMEM,
        compiler_params=params(),
        cost_estimate=pl.CostEstimate(flops=1000000, bytes_accessed=4000000, transcendentals=0),
        name="chip",
    )(tail, keep, recv)
    student_inputs = (student_rows, student_gain[None, :], student_weight)
    student_shapes = (
        jax.ShapeDtypeStruct((count, 2 * TILE), F32),
        jax.ShapeDtypeStruct((4 * DS, count), BF16),
    )
    student_scratch = [
        pltpu.VMEM(student_rows.shape, BF16),
        pltpu.VMEM((1, DS), F32),
        pltpu.VMEM(student_weight.shape, BF16),
        pltpu.VMEM((DS, count), BF16),
        pltpu.SemaphoreType.DMA((11,)),
    ]
    early, stash = pl.pallas_call(
        early_student_kernel,
        out_shape=student_shapes,
        in_specs=[HBM] * 3 + [VMEM],
        out_specs=(VMEM, HBM),
        scratch_shapes=student_scratch,
        compiler_params=params(52),
        cost_estimate=pl.CostEstimate(flops=2000000000, bytes_accessed=10000000, transcendentals=480),
        name="early_student",
    )(*student_inputs, line)
    early, stash, line = lax.optimization_barrier((early, stash, line))
    groups = [[z * 4 + x for x in range(4)] for z in range(2)]
    line = lax.all_to_all(line, "tp", 0, 0, tiled=True, axis_index_groups=groups)
    packed = pl.pallas_call(
        pack_kernel,
        out_shape=jax.ShapeDtypeStruct((2 * shards * PAD, TILE), BF16),
        in_specs=[VMEM] * 4,
        out_specs=HBM,
        scratch_shapes=[
            pltpu.VMEM((2 * shards * PAD, TILE), F32),
            pltpu.VMEM((2 * shards * PAD, TILE), BF16),
            pltpu.SemaphoreType.DMA((2,)),
        ],
        compiler_params=params(),
        cost_estimate=pl.CostEstimate(flops=400000000, bytes_accessed=2000000, transcendentals=0),
        name="pack",
    )(line, place, rank, hits)
    early, stash, packed = lax.optimization_barrier((early, stash, packed))
    student_out, stash, spread, own = pl.pallas_call(
        late_student_kernel,
        out_shape=(
            *student_shapes,
            jax.ShapeDtypeStruct((shards * PAD // 2, shards), BF16),
            jax.ShapeDtypeStruct((shards * PAD // 2, TILE), F32),
        ),
        in_specs=[HBM] * 3 + [VMEM, HBM],
        out_specs=(VMEM, HBM, VMEM, VMEM),
        input_output_aliases={4: 1},
        scratch_shapes=student_scratch,
        compiler_params=params(52),
        cost_estimate=pl.CostEstimate(flops=2000000000, bytes_accessed=10000000, transcendentals=480),
        name="late_student",
    )(*student_inputs, early, stash)
    groups = [
        [(g * 8 + z * 4 + x) * 2 + c for z in range(2) for g in range(shards)]
        for x in range(4)
        for c in range(2)
    ]
    arrived = lax.all_to_all(
        packed.reshape(2 * shards, PAD // 2, 2, TILE),
        ("grp", "tp", "role"),
        split_axis=0,
        concat_axis=0,
        tiled=True,
        axis_index_groups=groups,
    )
    rows = shards * PAD
    return pl.pallas_call(
        grad_kernel,
        out_shape=jax.ShapeDtypeStruct((DS, 2 * TILE), BF16),
        in_specs=[VMEM] * 4 + [HBM],
        out_specs=HBM,
        scratch_shapes=[
            pltpu.VMEM((2 * rows, TILE), F32),
            pltpu.VMEM((DS, count), BF16),
            pltpu.VMEM((DS, 2 * TILE), BF16),
            pltpu.SemaphoreType.DMA((2, 8)),
        ],
        compiler_params=params(52),
        cost_estimate=pl.CostEstimate(flops=1000000000, bytes_accessed=7000000, transcendentals=0),
        name="grad",
    )(arrived.reshape(2 * rows, TILE), student_out, spread, own, stash)


def solution(mesh):
    placed = (
        P("grp", ("tp", "role")),
        P(("tp", "role")),
        P(),
        P(("tp", "role"), None, None, None),
        P("grp", None),
        P("grp", None),
        P(),
        P(None, ("tp", "role")),
    )
    return jax.shard_map(
        on_device, mesh=mesh, in_specs=placed, out_specs=P("grp", ("tp", "role")), check_vma=False
    )
```

```python
import math

import jax
import jax.numpy as jnp
from jax import lax
from jax.experimental import pallas as pl
from jax.experimental.pallas import tpu as pltpu
from jax.sharding import PartitionSpec as P

DT = 16384
DS = 4096
TILE = 128
EPS = 1e-05
F32 = jnp.float32
BF16 = jnp.bfloat16
VMEM = pl.BlockSpec(memory_space=pltpu.VMEM)
HBM = pl.BlockSpec(memory_space=pltpu.HBM)
TOK = 256
CAP = 10
PAD = 22
TEACHER_MIB = 58
ROUTE_MIB = 46
STASH = 144
TAIL = 16


def params(mib=24):
    return pltpu.CompilerParams(vmem_limit_bytes=mib * 1024 * 1024)


def pack_sums(row):
    high = row.astype(BF16).astype(F32)
    low = row - high
    return jnp.concatenate([high, low, jnp.zeros((TAIL - 4, TILE), F32)], axis=0).astype(BF16)


def read_sums(tail):
    wide = tail.astype(F32)
    return wide[0:2] + wide[2:4]


def teacher_kernel(
    index_hbm, rows_hbm, gain_hbm, tiles_hbm, send_hbm, keep_hbm,
    index, rows, gain, tiles, acc, send, own_sums, sems
):
    first = [
        pltpu.make_async_copy(rows_hbm, rows, sems.at[8]),
        pltpu.make_async_copy(gain_hbm, gain, sems.at[9]),
        pltpu.make_async_copy(index_hbm, index, sems.at[10]),
    ]
    halves = [pl.ds(0, 4), pl.ds(4, 4)]
    loads = [
        pltpu.make_async_copy(tiles_hbm.at[part], tiles.at[part], sems.at[n])
        for n, part in enumerate(halves)
    ]
    for copy in first + loads:
        copy.start()
    role = lax.axis_index("role")
    base = (lax.axis_index("tp") * 2 + role) * 8
    acc[...] = jnp.zeros_like(acc)
    squares = jnp.zeros((TOK, TILE), F32)
    for copy in first:
        copy.wait()
    for b in range(8):
        lanes = slice(b * TILE, (b + 1) * TILE)
        wide = rows[:, lanes].astype(F32)
        squares = squares + wide * wide
        gained = (wide * gain[:, lanes]).astype(BF16)
        if b % 4 == 0:
            loads[b // 4].wait()
        side = jnp.concatenate([tiles[b, k] for k in range(8)], axis=1)
        products = jnp.dot(gained, side, preferred_element_type=F32)
        for k in range(8):
            c = index[k, base + b]
            own = 1 - jnp.bitwise_xor((c >> 1) & 1, role)
            place = own * 16 + ((c >> 2) & 3) * 4 + (c >> 4) * 2 + (c & 1)
            acc[place] += products[:, k * TILE : (k + 1) * TILE]
    stores = [
        pltpu.make_async_copy(acc.at[pl.ds(16, 16)], keep_hbm.at[pl.ds(0, 16)], sems.at[11])
    ]
    stores[0].start()
    sums = jnp.sum(squares, axis=1, keepdims=True) * (1.0 / DT)
    row = jnp.concatenate(
        [
            jnp.transpose(jnp.broadcast_to(sums[h * TILE : (h + 1) * TILE], (TILE, TILE)))[0:1]
            for h in range(2)
        ],
        axis=0,
    )
    own_sums[...] = jnp.concatenate([row, jnp.zeros((TAIL - 2, TILE), F32)], axis=0)
    stores.append(
        pltpu.make_async_copy(own_sums, keep_hbm.at[16, pl.ds(0, TAIL)], sems.at[16])
    )
    stores[1].start()
    send[16 * TOK :, :] = pack_sums(row)
    step = 4 * TOK
    for m in range(4):
        for n in range(4 * m, 4 * m + 4):
            send[n * TOK : (n + 1) * TOK, :] = acc[n].astype(BF16)
        here = pl.ds(m * step, step + (TAIL if m == 3 else 0))
        stores.append(pltpu.make_async_copy(send.at[here], send_hbm.at[here], sems.at[12 + m]))
        stores[-1].start()
    for copy in stores:
        copy.wait()


def chip_kernel(tail_ref, keep_ref, recv_ref, out_ref):
    tail = pack_sums(tail_ref[0:2] + read_sums(recv_ref[16 * TOK :, :]))
    for x in range(4):
        for n in range(4):
            m = x * 4 + n
            out_ref[x, n * TOK : (n + 1) * TOK, :] = (
                keep_ref[m] + recv_ref[m * TOK : (m + 1) * TOK, :].astype(F32)
            ).astype(BF16)
        out_ref[x, 4 * TOK :, :] = tail


def route_kernel(
    shard_ref, gain_ref, keep_hbm, place_ref, rank_ref, hits_ref, tail_ref, keep_ref, held_ref, sems
):
    copies = [
        pltpu.make_async_copy(keep_hbm.at[pl.ds(0, 16)], keep_ref, sems.at[0]),
        pltpu.make_async_copy(keep_hbm.at[16, pl.ds(0, TAIL)], tail_ref, sems.at[1]),
    ]
    for copy in copies:
        copy.start()
    held_ref[...] = gain_ref[...]
    dest = shard_ref[...]
    hits = jnp.where(lax.broadcasted_iota(jnp.int32, hits_ref.shape, 0) == dest, 1.0, 0.0)
    hits_ref[...] = hits.astype(BF16)
    earlier = jnp.where(
        lax.broadcasted_iota(jnp.int32, (TOK, TOK), 0)
        < lax.broadcasted_iota(jnp.int32, (TOK, TOK), 1),
        1.0,
        0.0,
    ).astype(BF16)
    counts = jnp.dot(hits.astype(BF16), earlier, preferred_element_type=F32)
    rank = jnp.sum(counts * hits, axis=0, keepdims=True).astype(jnp.int32)
    rank_ref[...] = jnp.broadcast_to(rank, rank_ref.shape)
    row = lax.broadcasted_iota(jnp.int32, (place_ref.shape[0], TOK), 0)
    for j in range(2):
        wanted = dest * PAD + 2 * rank + j
        place_ref[:, j * TOK : (j + 1) * TOK] = jnp.where(row == wanted, 1.0, 0.0).astype(BF16)
    for copy in copies:
        copy.wait()


def pack_kernel(recv_ref, place_ref, rank_ref, hits_ref, out_ref, wide):
    tail = slice(4 * TOK, 4 * TOK + TAIL)

    def total(n):
        part = [recv_ref[x, n * TOK : (n + 1) * TOK, :].astype(F32) for x in range(4)]
        return ((part[0] + part[1]) + (part[2] + part[3])).astype(BF16)

    sums = sum(read_sums(recv_ref[x, tail, :]) for x in range(4))
    sums = jnp.concatenate([sums[0:1], sums[1:2]], axis=1)
    high = sums.astype(BF16).astype(F32)
    slot = lax.broadcasted_iota(jnp.int32, (TILE, TOK), 0) == rank_ref[0:1, :]
    rows = place_ref.shape[0]
    parts = jnp.concatenate(
        [jnp.concatenate([total(z * 2 + j) for z in range(2)], axis=1) for j in range(2)], axis=0
    )
    moved = jnp.dot(place_ref[...], parts, preferred_element_type=F32)
    for z in range(2):
        wide[z * rows : (z + 1) * rows, :] = moved[:, z * TILE : (z + 1) * TILE]
    for n, values in enumerate((high, sums - high)):
        held = jnp.where(slot, values, 0.0).astype(BF16)
        shown = lax.dot_general(
            hits_ref[...], held, (((1,), (1,)), ((), ())), preferred_element_type=F32
        )
        for z in range(2):
            wide[pl.ds(z * rows + 2 * CAP + n, shown.shape[0], stride=PAD), :] = shown
    out_ref[...] = wide[...].astype(BF16)


def student_work(rows_hbm, gain, weight_hbm, out_ref, stash_hbm, rows, weight, turned, sems):
    steps = 8
    step = DS // steps
    loads = [
        pltpu.make_async_copy(rows_hbm, rows, sems.at[steps]),
        pltpu.make_async_copy(weight_hbm, weight, sems.at[steps + 1]),
    ]
    for copy in loads:
        copy.start()
    count = rows.shape[0]
    squares = jnp.zeros((count, TILE), F32)
    loads[0].wait()
    for n in range(DS // TILE):
        wide = rows[:, n * TILE : (n + 1) * TILE].astype(F32)
        squares = squares + wide * wide
    scale = lax.rsqrt(jnp.sum(squares, axis=1, keepdims=True) / DS + EPS)
    out_ref[...] = jnp.zeros_like(out_ref)
    loads[1].wait()
    copies = []
    for n in range(steps):
        part = slice(n * step, (n + 1) * step)
        normed = (rows[:, part].astype(F32) * scale * gain[:, part]).astype(BF16)
        out_ref[...] += jnp.dot(normed, weight[part, :], preferred_element_type=F32)
        turned[part, :] = jnp.transpose(normed)
        here = pl.ds(n * step, step)
        copies.append(pltpu.make_async_copy(turned.at[here], stash_hbm.at[here], sems.at[n]))
        copies[n].start()
    for copy in copies:
        copy.wait()


def early_student_kernel(rows_hbm, gain_ref, weight_hbm, line_ref, out_ref, stash_hbm, *scratch):
    @pl.when(lax.axis_index("role") == 0)
    def _():
        student_work(rows_hbm, gain_ref, weight_hbm, out_ref, stash_hbm, *scratch)


def late_student_kernel(
    rows_hbm, gain_ref, weight_hbm, recv_ref, early_hbm, out_ref, stash_hbm, *scratch
):
    @pl.when(lax.axis_index("role") == 1)
    def _():
        student_work(rows_hbm, gain_ref, weight_hbm, out_ref, stash_hbm, *scratch)


def grad_kernel(
    recv_ref, early_ref, late_ref, stash_hbm, grad_hbm, wide, turned, grad, sems
):
    steps = sems.shape[1]
    block = DS // steps
    here = [pl.ds(n * block, block) for n in range(steps)]
    loads = {
        n: pltpu.make_async_copy(
            stash_hbm.at[pl.ds(n * block, size * block)],
            turned.at[pl.ds(n * block, size * block)],
            sems.at[0, n],
        )
        for n, size in ((0, 1), (1, 3), (4, 4))
    }
    stores = [
        pltpu.make_async_copy(grad.at[here[n]], grad_hbm.at[here[n]], sems.at[1, n])
        for n in range(steps)
    ]
    for copy in loads.values():
        copy.start()
    half = wide.shape[0] // 2
    count = half // 2
    shards = half // PAD
    row = lax.broadcasted_iota(jnp.int32, (count, 1), 0)
    source = row // (PAD // 2)
    own = lax.broadcasted_iota(jnp.int32, (count, TILE), 1) == row - source * (PAD // 2)
    spread = jnp.where(
        lax.broadcasted_iota(jnp.int32, (count, shards), 1) == source, 1.0, 0.0
    ).astype(BF16)
    row = lax.broadcasted_iota(jnp.int32, (1, count), 1)
    source = row // (PAD // 2)
    row = jnp.where(row - source * (PAD // 2) < CAP, row - source, -1)
    pick = jnp.where(
        lax.broadcasted_iota(jnp.int32, (early_ref.shape[0], count), 0) == row, 1.0, 0.0
    ).astype(BF16)
    wide[...] = recv_ref[...].astype(F32)

    def every(start, size, stride):
        return sum(wide[pl.ds(z * half + start, size, stride=stride), :] for z in range(2))

    sums = every(2 * CAP, shards, PAD) + every(2 * CAP + 1, shards, PAD)
    inv = lax.rsqrt(sums + EPS)
    high = inv.astype(BF16)
    low = (inv - high.astype(F32)).astype(BF16)
    rows = jnp.dot(
        spread, jnp.concatenate([high, low], axis=1), preferred_element_type=F32
    )
    scale = jnp.sum(
        jnp.where(own, rows[:, :TILE] + rows[:, TILE:], 0.0), axis=1, keepdims=True
    )
    targets = jnp.concatenate(
        [(scale * every(j, count, 2)).astype(BF16) for j in range(2)], axis=1
    )
    wanted = jnp.dot(pick, targets, preferred_element_type=F32)
    student_out = jnp.where(lax.axis_index("role") == 0, early_ref[...], late_ref[...])
    delta = ((student_out - wanted) * (1.0 / math.sqrt(TOK))).astype(BF16)
    for n in range(steps):
        if n in loads:
            loads[n].wait()
        grad[here[n], :] = jnp.dot(
            turned[here[n], :], delta, preferred_element_type=F32
        ).astype(BF16)
        stores[n].start()
    for copy in stores:
        copy.wait()


def on_device(
    teacher_rows,
    teacher_gain,
    block_index,
    block_tiles,
    student_shard,
    student_rows,
    student_gain,
    student_weight,
):
    shards = lax.axis_size("grp")
    count = student_rows.shape[0]
    send, keep = pl.pallas_call(
        teacher_kernel,
        out_shape=(
            jax.ShapeDtypeStruct((16 * TOK + TAIL, TILE), BF16),
            jax.ShapeDtypeStruct((STASH, TOK, TILE), F32),
        ),
        in_specs=[HBM] * 4,
        out_specs=(HBM, HBM),
        scratch_shapes=[
            pltpu.SMEM((8, TILE), jnp.int32),
            pltpu.VMEM(teacher_rows.shape, BF16),
            pltpu.VMEM((1, teacher_rows.shape[1]), F32),
            pltpu.VMEM(block_tiles.shape, BF16),
            pltpu.VMEM((32, TOK, TILE), F32),
            pltpu.VMEM((16 * TOK + TAIL, TILE), BF16),
            pltpu.VMEM((TAIL, TILE), F32),
            pltpu.SemaphoreType.DMA((17,)),
        ],
        compiler_params=params(TEACHER_MIB),
        cost_estimate=pl.CostEstimate(flops=540000000, bytes_accessed=6000000, transcendentals=0),
        name="teacher",
    )(block_index.T, teacher_rows, teacher_gain[None, :], block_tiles)
    recv = lax.ppermute(send, "role", [(0, 1), (1, 0)])
    student_shard, student_gain, keep = lax.optimization_barrier(
        (student_shard, student_gain, keep)
    )
    place, rank, hits, tail, keep, gain = pl.pallas_call(
        route_kernel,
        out_shape=(
            jax.ShapeDtypeStruct((shards * PAD, 2 * TOK), BF16),
            jax.ShapeDtypeStruct((8, TOK), jnp.int32),
            jax.ShapeDtypeStruct((shards, TOK), BF16),
            jax.ShapeDtypeStruct((TAIL, TILE), F32),
            jax.ShapeDtypeStruct((16, TOK, TILE), F32),
            jax.ShapeDtypeStruct((1, DS), F32),
        ),
        in_specs=[VMEM, VMEM, HBM],
        out_specs=(VMEM,) * 6,
        scratch_shapes=[pltpu.SemaphoreType.DMA((2,))],
        compiler_params=params(ROUTE_MIB),
        cost_estimate=pl.CostEstimate(flops=100000000, bytes_accessed=4000000, transcendentals=0),
        name="route",
    )(student_shard.reshape(1, TOK), student_gain[None, :], keep)
    place, rank, hits, tail, keep, gain, recv = lax.optimization_barrier(
        (place, rank, hits, tail, keep, gain, recv)
    )
    line = pl.pallas_call(
        chip_kernel,
        out_shape=jax.ShapeDtypeStruct((4, 4 * TOK + TAIL, TILE), BF16),
        in_specs=[VMEM] * 3,
        out_specs=VMEM,
        compiler_params=params(),
        cost_estimate=pl.CostEstimate(flops=1000000, bytes_accessed=4000000, transcendentals=0),
        name="chip",
    )(tail, keep, recv)
    student_inputs = (student_rows, gain, student_weight)
    student_shapes = (
        jax.ShapeDtypeStruct((count, 2 * TILE), F32),
        jax.ShapeDtypeStruct((4 * DS, count), BF16),
    )
    student_scratch = [
        pltpu.VMEM(student_rows.shape, BF16),
        pltpu.VMEM(student_weight.shape, BF16),
        pltpu.VMEM((DS, count), BF16),
        pltpu.SemaphoreType.DMA((10,)),
    ]
    early, stash = pl.pallas_call(
        early_student_kernel,
        out_shape=student_shapes,
        in_specs=[HBM, VMEM, HBM, VMEM],
        out_specs=(VMEM, HBM),
        scratch_shapes=student_scratch,
        compiler_params=params(52),
        cost_estimate=pl.CostEstimate(flops=2000000000, bytes_accessed=10000000, transcendentals=480),
        name="early_student",
    )(*student_inputs, line)
    early, stash, line = lax.optimization_barrier((early, stash, line))
    groups = [[z * 4 + x for x in range(4)] for z in range(2)]
    line = lax.all_to_all(line, "tp", 0, 0, tiled=True, axis_index_groups=groups)
    packed = pl.pallas_call(
        pack_kernel,
        out_shape=jax.ShapeDtypeStruct((2 * shards * PAD, TILE), BF16),
        in_specs=[VMEM] * 4,
        out_specs=VMEM,
        scratch_shapes=[pltpu.VMEM((2 * shards * PAD, TILE), F32)],
        compiler_params=params(),
        cost_estimate=pl.CostEstimate(flops=400000000, bytes_accessed=2000000, transcendentals=0),
        name="pack",
    )(line, place, rank, hits)
    groups = [
        [(g * 8 + z * 4 + x) * 2 + c for z in range(2) for g in range(shards)]
        for x in range(4)
        for c in range(2)
    ]
    arrived = lax.all_to_all(
        packed.reshape(2 * shards, PAD // 2, 2, TILE),
        ("grp", "tp", "role"),
        split_axis=0,
        concat_axis=0,
        tiled=True,
        axis_index_groups=groups,
    )
    rows = shards * PAD
    arrived = arrived.reshape(2 * rows, TILE)
    late, stash = pl.pallas_call(
        late_student_kernel,
        out_shape=student_shapes,
        in_specs=[HBM, VMEM, HBM, VMEM, HBM],
        out_specs=(VMEM, HBM),
        input_output_aliases={4: 1},
        scratch_shapes=student_scratch,
        compiler_params=params(52),
        cost_estimate=pl.CostEstimate(flops=2000000000, bytes_accessed=10000000, transcendentals=480),
        name="late_student",
    )(*student_inputs, arrived, stash)
    return pl.pallas_call(
        grad_kernel,
        out_shape=jax.ShapeDtypeStruct((DS, 2 * TILE), BF16),
        in_specs=[VMEM] * 3 + [HBM],
        out_specs=HBM,
        scratch_shapes=[
            pltpu.VMEM((2 * rows, TILE), F32),
            pltpu.VMEM((DS, count), BF16),
            pltpu.VMEM((DS, 2 * TILE), BF16),
            pltpu.SemaphoreType.DMA((2, 8)),
        ],
        compiler_params=params(52),
        cost_estimate=pl.CostEstimate(flops=1000000000, bytes_accessed=7000000, transcendentals=0),
        name="grad",
    )(arrived, early, late, stash)


def solution(mesh):
    placed = (
        P("grp", ("tp", "role")),
        P(("tp", "role")),
        P(),
        P(("tp", "role"), None, None, None),
        P("grp", None),
        P("grp", None),
        P(),
        P(None, ("tp", "role")),
    )
    return jax.shard_map(
        on_device, mesh=mesh, in_specs=placed, out_specs=P("grp", ("tp", "role")), check_vma=False
    )
```

```python
import math

import jax
import jax.numpy as jnp
from jax import lax
from jax.experimental import pallas as pl
from jax.experimental.pallas import tpu as pltpu
from jax.sharding import PartitionSpec as P

DT = 16384
DS = 4096
TILE = 128
EPS = 1e-05
F32 = jnp.float32
BF16 = jnp.bfloat16
VMEM = pl.BlockSpec(memory_space=pltpu.VMEM)
HBM = pl.BlockSpec(memory_space=pltpu.HBM)
TOK = 256
CAP = 10
PAD = 22
TEACHER_MIB = 58
ROUTE_MIB = 46
STASH = 144
TAIL = 16


def params(mib=24):
    return pltpu.CompilerParams(vmem_limit_bytes=mib * 1024 * 1024)


def pack_sums(row):
    high = row.astype(BF16).astype(F32)
    low = row - high
    return jnp.concatenate([high, low, jnp.zeros((TAIL - 4, TILE), F32)], axis=0).astype(BF16)


def read_sums(tail):
    wide = tail.astype(F32)
    return wide[0:2] + wide[2:4]


def teacher_kernel(
    index_hbm, rows_hbm, gain_hbm, tiles_hbm, send_hbm, keep_hbm,
    index, rows, gain, tiles, acc, send, own_sums, sems
):
    first = [
        pltpu.make_async_copy(rows_hbm, rows, sems.at[8]),
        pltpu.make_async_copy(gain_hbm, gain, sems.at[9]),
        pltpu.make_async_copy(index_hbm, index, sems.at[10]),
    ]
    halves = [pl.ds(0, 4), pl.ds(4, 4)]
    loads = [
        pltpu.make_async_copy(tiles_hbm.at[part], tiles.at[part], sems.at[n])
        for n, part in enumerate(halves)
    ]
    for copy in first + loads:
        copy.start()
    role = lax.axis_index("role")
    base = (lax.axis_index("tp") * 2 + role) * 8
    acc[...] = jnp.zeros_like(acc)
    squares = jnp.zeros((TOK, TILE), F32)
    for copy in first:
        copy.wait()
    for b in range(8):
        lanes = slice(b * TILE, (b + 1) * TILE)
        wide = rows[:, lanes].astype(F32)
        squares = squares + wide * wide
        gained = (wide * gain[:, lanes]).astype(BF16)
        if b % 4 == 0:
            loads[b // 4].wait()
        side = jnp.concatenate([tiles[b, k] for k in range(8)], axis=1)
        products = jnp.dot(gained, side, preferred_element_type=F32)
        for k in range(8):
            c = index[k, base + b]
            own = 1 - jnp.bitwise_xor((c >> 1) & 1, role)
            place = own * 16 + ((c >> 2) & 3) * 4 + (c >> 4) * 2 + (c & 1)
            acc[place] += products[:, k * TILE : (k + 1) * TILE]
    stores = [
        pltpu.make_async_copy(acc.at[pl.ds(16, 16)], keep_hbm.at[pl.ds(0, 16)], sems.at[11])
    ]
    stores[0].start()
    sums = jnp.sum(squares, axis=1, keepdims=True) * (1.0 / DT)
    row = jnp.concatenate(
        [
            jnp.transpose(jnp.broadcast_to(sums[h * TILE : (h + 1) * TILE], (TILE, TILE)))[0:1]
            for h in range(2)
        ],
        axis=0,
    )
    own_sums[...] = jnp.concatenate([row, jnp.zeros((TAIL - 2, TILE), F32)], axis=0)
    stores.append(
        pltpu.make_async_copy(own_sums, keep_hbm.at[16, pl.ds(0, TAIL)], sems.at[16])
    )
    stores[1].start()
    send[16 * TOK :, :] = pack_sums(row)
    step = 4 * TOK
    for m in range(4):
        for n in range(4 * m, 4 * m + 4):
            send[n * TOK : (n + 1) * TOK, :] = acc[n].astype(BF16)
        here = pl.ds(m * step, step + (TAIL if m == 3 else 0))
        stores.append(pltpu.make_async_copy(send.at[here], send_hbm.at[here], sems.at[12 + m]))
        stores[-1].start()
    for copy in stores:
        copy.wait()


def chip_kernel(tail_ref, keep_ref, recv_ref, out_ref):
    tail = pack_sums(tail_ref[0:2] + read_sums(recv_ref[16 * TOK :, :]))
    for x in range(4):
        for n in range(4):
            m = x * 4 + n
            out_ref[x, n * TOK : (n + 1) * TOK, :] = (
                keep_ref[m] + recv_ref[m * TOK : (m + 1) * TOK, :].astype(F32)
            ).astype(BF16)
        out_ref[x, 4 * TOK :, :] = tail


def route_kernel(
    shard_ref, gain_ref, keep_hbm, place_ref, rank_ref, hits_ref, tail_ref, keep_ref, held_ref, sems
):
    copies = [
        pltpu.make_async_copy(keep_hbm.at[pl.ds(0, 16)], keep_ref, sems.at[0]),
        pltpu.make_async_copy(keep_hbm.at[16, pl.ds(0, TAIL)], tail_ref, sems.at[1]),
    ]
    for copy in copies:
        copy.start()
    held_ref[...] = gain_ref[...]
    dest = shard_ref[...]
    hits = jnp.where(lax.broadcasted_iota(jnp.int32, hits_ref.shape, 0) == dest, 1.0, 0.0)
    hits_ref[...] = hits.astype(BF16)
    earlier = jnp.where(
        lax.broadcasted_iota(jnp.int32, (TOK, TOK), 0)
        < lax.broadcasted_iota(jnp.int32, (TOK, TOK), 1),
        1.0,
        0.0,
    ).astype(BF16)
    counts = jnp.dot(hits.astype(BF16), earlier, preferred_element_type=F32)
    rank = jnp.sum(counts * hits, axis=0, keepdims=True).astype(jnp.int32)
    rank_ref[...] = jnp.broadcast_to(rank, rank_ref.shape)
    row = lax.broadcasted_iota(jnp.int32, (place_ref.shape[0], TOK), 0)
    for j in range(2):
        wanted = dest * PAD + 2 * rank + j
        place_ref[:, j * TOK : (j + 1) * TOK] = jnp.where(row == wanted, 1.0, 0.0).astype(BF16)
    for copy in copies:
        copy.wait()


def pack_kernel(recv_ref, place_ref, rank_ref, hits_ref, out_ref, wide):
    tail = slice(4 * TOK, 4 * TOK + TAIL)

    def total(n):
        part = [recv_ref[x, n * TOK : (n + 1) * TOK, :].astype(F32) for x in range(4)]
        return ((part[0] + part[1]) + (part[2] + part[3])).astype(BF16)

    sums = sum(read_sums(recv_ref[x, tail, :]) for x in range(4))
    sums = jnp.concatenate([sums[0:1], sums[1:2]], axis=1)
    high = sums.astype(BF16).astype(F32)
    slot = lax.broadcasted_iota(jnp.int32, (TILE, TOK), 0) == rank_ref[0:1, :]
    rows = place_ref.shape[0]
    parts = jnp.concatenate(
        [jnp.concatenate([total(z * 2 + j) for z in range(2)], axis=1) for j in range(2)], axis=0
    )
    moved = jnp.dot(place_ref[...], parts, preferred_element_type=F32)
    for z in range(2):
        wide[z * rows : (z + 1) * rows, :] = moved[:, z * TILE : (z + 1) * TILE]
    for n, values in enumerate((high, sums - high)):
        held = jnp.where(slot, values, 0.0).astype(BF16)
        shown = lax.dot_general(
            hits_ref[...], held, (((1,), (1,)), ((), ())), preferred_element_type=F32
        )
        for z in range(2):
            wide[pl.ds(z * rows + 2 * CAP + n, shown.shape[0], stride=PAD), :] = shown
    out_ref[...] = wide[: 2 * rows, :].astype(BF16)


def student_work(rows_hbm, gain, weight_hbm, out_ref, stash_hbm, rows, weight, turned, sems):
    steps = 8
    step = DS // steps
    loads = [
        pltpu.make_async_copy(rows_hbm, rows, sems.at[steps]),
        pltpu.make_async_copy(weight_hbm, weight, sems.at[steps + 1]),
    ]
    for copy in loads:
        copy.start()
    count = rows.shape[0]
    squares = jnp.zeros((count, TILE), F32)
    loads[0].wait()
    for n in range(DS // TILE):
        wide = rows[:, n * TILE : (n + 1) * TILE].astype(F32)
        squares = squares + wide * wide
    scale = lax.rsqrt(jnp.sum(squares, axis=1, keepdims=True) / DS + EPS)
    out_ref[...] = jnp.zeros_like(out_ref)
    loads[1].wait()
    copies = []
    for n in range(steps):
        part = slice(n * step, (n + 1) * step)
        normed = (rows[:, part].astype(F32) * scale * gain[:, part]).astype(BF16)
        out_ref[...] += jnp.dot(normed, weight[part, :], preferred_element_type=F32)
        turned[part, :] = jnp.transpose(normed)
        here = pl.ds(n * step, step)
        copies.append(pltpu.make_async_copy(turned.at[here], stash_hbm.at[here], sems.at[n]))
        copies[n].start()
    for copy in copies:
        copy.wait()


def early_student_kernel(
    rows_hbm, gain_ref, weight_hbm, line_ref, out_ref, stash_hbm, head_ref, rows, weight, turned, sems
):
    @pl.when(lax.axis_index("role") == 0)
    def _():
        student_work(
            rows_hbm, gain_ref, weight_hbm, out_ref, stash_hbm, rows, weight, turned, sems
        )
        head_ref[...] = turned[: head_ref.shape[0], :]


def late_student_kernel(
    rows_hbm, gain_ref, weight_hbm, recv_ref, early_hbm, out_ref, stash_hbm, *scratch
):
    @pl.when(lax.axis_index("role") == 1)
    def _():
        student_work(rows_hbm, gain_ref, weight_hbm, out_ref, stash_hbm, *scratch)


def grad_kernel(
    recv_ref, early_ref, late_ref, head_ref, stash_hbm, grad_hbm, wide, turned, grad, sems
):
    steps = sems.shape[1]
    block = DS // steps
    here = [pl.ds(n * block, block) for n in range(steps)]
    loads = {
        n: pltpu.make_async_copy(
            stash_hbm.at[pl.ds(n * block, size * block)],
            turned.at[pl.ds(n * block, size * block)],
            sems.at[0, n],
        )
        for n, size in ((0, 1), (1, 3), (4, 4))
    }
    stores = [
        pltpu.make_async_copy(grad.at[here[n]], grad_hbm.at[here[n]], sems.at[1, n])
        for n in range(steps)
    ]
    early_core = lax.axis_index("role") == 0
    for n, copy in loads.items():
        if n:
            copy.start()

    @pl.when(jnp.logical_not(early_core))
    def _():
        loads[0].start()

    @pl.when(early_core)
    def _():
        turned[:block, :] = head_ref[...]

    half = recv_ref.shape[0] // 2
    count = half // 2
    shards = half // PAD
    row = lax.broadcasted_iota(jnp.int32, (count, 1), 0)
    source = row // (PAD // 2)
    own = lax.broadcasted_iota(jnp.int32, (count, TILE), 1) == row - source * (PAD // 2)
    spread = jnp.where(
        lax.broadcasted_iota(jnp.int32, (count, shards), 1) == source, 1.0, 0.0
    ).astype(BF16)
    row = lax.broadcasted_iota(jnp.int32, (1, count), 1)
    source = row // (PAD // 2)
    row = jnp.where(row - source * (PAD // 2) < CAP, row - source, -1)
    pick = jnp.where(
        lax.broadcasted_iota(jnp.int32, (early_ref.shape[0], count), 0) == row, 1.0, 0.0
    ).astype(BF16)
    wide[: 2 * half, :] = recv_ref[...].astype(F32)

    def every(start, size, stride):
        return sum(wide[pl.ds(z * half + start, size, stride=stride), :] for z in range(2))

    sums = every(2 * CAP, shards, PAD) + every(2 * CAP + 1, shards, PAD)
    inv = lax.rsqrt(sums + EPS)
    high = inv.astype(BF16)
    low = (inv - high.astype(F32)).astype(BF16)
    rows = jnp.dot(
        spread, jnp.concatenate([high, low], axis=1), preferred_element_type=F32
    )
    scale = jnp.sum(
        jnp.where(own, rows[:, :TILE] + rows[:, TILE:], 0.0), axis=1, keepdims=True
    )
    targets = jnp.concatenate(
        [(scale * every(j, count, 2)).astype(BF16) for j in range(2)], axis=1
    )
    wanted = jnp.dot(pick, targets, preferred_element_type=F32)
    student_out = jnp.where(early_core, early_ref[...], late_ref[...])
    delta = ((student_out - wanted) * (1.0 / math.sqrt(TOK))).astype(BF16)

    @pl.when(jnp.logical_not(early_core))
    def _():
        loads[0].wait()

    for n in range(steps):
        if n and n in loads:
            loads[n].wait()
        grad[here[n], :] = jnp.dot(
            turned[here[n], :], delta, preferred_element_type=F32
        ).astype(BF16)
        stores[n].start()
    for copy in stores:
        copy.wait()


def on_device(
    teacher_rows,
    teacher_gain,
    block_index,
    block_tiles,
    student_shard,
    student_rows,
    student_gain,
    student_weight,
):
    shards = lax.axis_size("grp")
    count = student_rows.shape[0]
    send, keep = pl.pallas_call(
        teacher_kernel,
        out_shape=(
            jax.ShapeDtypeStruct((16 * TOK + TAIL, TILE), BF16),
            jax.ShapeDtypeStruct((STASH, TOK, TILE), F32),
        ),
        in_specs=[HBM] * 4,
        out_specs=(HBM, HBM),
        scratch_shapes=[
            pltpu.SMEM((8, TILE), jnp.int32),
            pltpu.VMEM(teacher_rows.shape, BF16),
            pltpu.VMEM((1, teacher_rows.shape[1]), F32),
            pltpu.VMEM(block_tiles.shape, BF16),
            pltpu.VMEM((32, TOK, TILE), F32),
            pltpu.VMEM((16 * TOK + TAIL, TILE), BF16),
            pltpu.VMEM((TAIL, TILE), F32),
            pltpu.SemaphoreType.DMA((17,)),
        ],
        compiler_params=params(TEACHER_MIB),
        cost_estimate=pl.CostEstimate(flops=540000000, bytes_accessed=6000000, transcendentals=0),
        name="teacher",
    )(block_index.T, teacher_rows, teacher_gain[None, :], block_tiles)
    recv = lax.ppermute(send, "role", [(0, 1), (1, 0)])
    student_shard, student_gain, keep = lax.optimization_barrier(
        (student_shard, student_gain, keep)
    )
    place, rank, hits, tail, keep, gain = pl.pallas_call(
        route_kernel,
        out_shape=(
            jax.ShapeDtypeStruct((shards * PAD, 2 * TOK), BF16),
            jax.ShapeDtypeStruct((8, TOK), jnp.int32),
            jax.ShapeDtypeStruct((shards, TOK), BF16),
            jax.ShapeDtypeStruct((TAIL, TILE), F32),
            jax.ShapeDtypeStruct((16, TOK, TILE), F32),
            jax.ShapeDtypeStruct((1, DS), F32),
        ),
        in_specs=[VMEM, VMEM, HBM],
        out_specs=(VMEM,) * 6,
        scratch_shapes=[pltpu.SemaphoreType.DMA((2,))],
        compiler_params=params(ROUTE_MIB),
        cost_estimate=pl.CostEstimate(flops=100000000, bytes_accessed=4000000, transcendentals=0),
        name="route",
    )(student_shard.reshape(1, TOK), student_gain[None, :], keep)
    place, rank, hits, tail, keep, gain, recv = lax.optimization_barrier(
        (place, rank, hits, tail, keep, gain, recv)
    )
    line = pl.pallas_call(
        chip_kernel,
        out_shape=jax.ShapeDtypeStruct((4, 4 * TOK + TAIL, TILE), BF16),
        in_specs=[VMEM] * 3,
        out_specs=VMEM,
        compiler_params=params(),
        cost_estimate=pl.CostEstimate(flops=1000000, bytes_accessed=4000000, transcendentals=0),
        name="chip",
    )(tail, keep, recv)
    student_inputs = (student_rows, gain, student_weight)
    student_shapes = (
        jax.ShapeDtypeStruct((count, 2 * TILE), F32),
        jax.ShapeDtypeStruct((4 * DS, count), BF16),
    )
    student_scratch = [
        pltpu.VMEM(student_rows.shape, BF16),
        pltpu.VMEM(student_weight.shape, BF16),
        pltpu.VMEM((DS, count), BF16),
        pltpu.SemaphoreType.DMA((10,)),
    ]
    early, stash, head = pl.pallas_call(
        early_student_kernel,
        out_shape=(*student_shapes, jax.ShapeDtypeStruct((DS // 8, count), BF16)),
        in_specs=[HBM, VMEM, HBM, VMEM],
        out_specs=(VMEM, HBM, VMEM),
        scratch_shapes=student_scratch,
        compiler_params=params(51),
        cost_estimate=pl.CostEstimate(flops=2000000000, bytes_accessed=10000000, transcendentals=480),
        name="early_student",
    )(*student_inputs, line)
    early, stash, head, line = lax.optimization_barrier((early, stash, head, line))
    groups = [[z * 4 + x for x in range(4)] for z in range(2)]
    line = lax.all_to_all(line, "tp", 0, 0, tiled=True, axis_index_groups=groups)
    packed = pl.pallas_call(
        pack_kernel,
        out_shape=jax.ShapeDtypeStruct((2 * shards * PAD, TILE), BF16),
        in_specs=[VMEM] * 4,
        out_specs=VMEM,
        scratch_shapes=[pltpu.VMEM((2 * shards * PAD + 2 * TAIL, TILE), F32)],
        compiler_params=params(),
        cost_estimate=pl.CostEstimate(flops=400000000, bytes_accessed=2000000, transcendentals=0),
        name="pack",
    )(line, place, rank, hits)
    groups = [
        [(g * 8 + z * 4 + x) * 2 + c for z in range(2) for g in range(shards)]
        for x in range(4)
        for c in range(2)
    ]
    arrived = lax.all_to_all(
        packed.reshape(2 * shards, PAD // 2, 2, TILE),
        ("grp", "tp", "role"),
        split_axis=0,
        concat_axis=0,
        tiled=True,
        axis_index_groups=groups,
    )
    rows = shards * PAD
    arrived = arrived.reshape(2 * rows, TILE)
    late, stash = pl.pallas_call(
        late_student_kernel,
        out_shape=student_shapes,
        in_specs=[HBM, VMEM, HBM, VMEM, HBM],
        out_specs=(VMEM, HBM),
        input_output_aliases={4: 1},
        scratch_shapes=student_scratch,
        compiler_params=params(51),
        cost_estimate=pl.CostEstimate(flops=2000000000, bytes_accessed=10000000, transcendentals=480),
        name="late_student",
    )(*student_inputs, arrived, stash)
    return pl.pallas_call(
        grad_kernel,
        out_shape=jax.ShapeDtypeStruct((DS, 2 * TILE), BF16),
        in_specs=[VMEM] * 4 + [HBM],
        out_specs=HBM,
        scratch_shapes=[
            pltpu.VMEM((2 * rows + 2 * TAIL, TILE), F32),
            pltpu.VMEM((DS, count), BF16),
            pltpu.VMEM((DS, 2 * TILE), BF16),
            pltpu.SemaphoreType.DMA((2, 8)),
        ],
        compiler_params=params(51),
        cost_estimate=pl.CostEstimate(flops=1000000000, bytes_accessed=7000000, transcendentals=0),
        name="grad",
    )(arrived, early, late, head, stash)


def solution(mesh):
    placed = (
        P("grp", ("tp", "role")),
        P(("tp", "role")),
        P(),
        P(("tp", "role"), None, None, None),
        P("grp", None),
        P("grp", None),
        P(),
        P(None, ("tp", "role")),
    )
    return jax.shard_map(
        on_device, mesh=mesh, in_specs=placed, out_specs=P("grp", ("tp", "role")), check_vma=False
    )
```

```python
import math

import jax
import jax.numpy as jnp
from jax import lax
from jax.experimental import pallas as pl
from jax.experimental.pallas import tpu as pltpu
from jax.sharding import PartitionSpec as P

DT = 16384
DS = 4096
TILE = 128
EPS = 1e-05
F32 = jnp.float32
BF16 = jnp.bfloat16
VMEM = pl.BlockSpec(memory_space=pltpu.VMEM)
HBM = pl.BlockSpec(memory_space=pltpu.HBM)
TOK = 256
CAP = 10
PAD = 22
TEACHER_MIB = 58
ROUTE_MIB = 46
STASH = 288
TAIL = 16


def params(mib=24):
    return pltpu.CompilerParams(vmem_limit_bytes=mib * 1024 * 1024)


def pack_sums(row):
    high = row.astype(BF16).astype(F32)
    low = row - high
    return jnp.concatenate([high, low, jnp.zeros((TAIL - 4, TILE), F32)], axis=0).astype(BF16)


def read_sums(tail):
    wide = tail.astype(F32)
    return wide[0:2] + wide[2:4]


def teacher_kernel(
    index_hbm, rows_hbm, gain_hbm, tiles_hbm, send_hbm, keep_hbm,
    index, rows, gain, tiles, acc, send, held, own_sums, sems
):
    first = [
        pltpu.make_async_copy(rows_hbm, rows, sems.at[8]),
        pltpu.make_async_copy(gain_hbm, gain, sems.at[9]),
        pltpu.make_async_copy(index_hbm, index, sems.at[10]),
    ]
    halves = [pl.ds(0, 4), pl.ds(4, 4)]
    loads = [
        pltpu.make_async_copy(tiles_hbm.at[part], tiles.at[part], sems.at[n])
        for n, part in enumerate(halves)
    ]
    for copy in first + loads:
        copy.start()
    role = lax.axis_index("role")
    base = (lax.axis_index("tp") * 2 + role) * 8
    acc[...] = jnp.zeros_like(acc)
    squares = jnp.zeros((TOK, TILE), F32)
    for copy in first:
        copy.wait()
    for b in range(8):
        lanes = slice(b * TILE, (b + 1) * TILE)
        wide = rows[:, lanes].astype(F32)
        squares = squares + wide * wide
        gained = (wide * gain[:, lanes]).astype(BF16)
        if b % 4 == 0:
            loads[b // 4].wait()
        side = jnp.concatenate([tiles[b, k] for k in range(8)], axis=1)
        products = jnp.dot(gained, side, preferred_element_type=F32)
        for k in range(8):
            c = index[k, base + b]
            own = 1 - jnp.bitwise_xor((c >> 1) & 1, role)
            place = own * 16 + ((c >> 2) & 3) * 4 + (c >> 4) * 2 + (c & 1)
            acc[place] += products[:, k * TILE : (k + 1) * TILE]
    for n in range(16):
        held[n] = acc[16 + n].astype(BF16)
    stores = [pltpu.make_async_copy(held, keep_hbm.at[pl.ds(0, 16)], sems.at[11])]
    stores[0].start()
    sums = jnp.sum(squares, axis=1, keepdims=True) * (1.0 / DT)
    row = jnp.concatenate(
        [
            jnp.transpose(jnp.broadcast_to(sums[h * TILE : (h + 1) * TILE], (TILE, TILE)))[0:1]
            for h in range(2)
        ],
        axis=0,
    )
    own_sums[...] = pack_sums(row)
    stores.append(
        pltpu.make_async_copy(own_sums, keep_hbm.at[16, pl.ds(0, TAIL)], sems.at[16])
    )
    stores[1].start()
    send[16 * TOK :, :] = pack_sums(row)
    step = 4 * TOK
    for m in range(4):
        for n in range(4 * m, 4 * m + 4):
            send[n * TOK : (n + 1) * TOK, :] = acc[n].astype(BF16)
        here = pl.ds(m * step, step + (TAIL if m == 3 else 0))
        stores.append(pltpu.make_async_copy(send.at[here], send_hbm.at[here], sems.at[12 + m]))
        stores[-1].start()
    for copy in stores:
        copy.wait()


def chip_kernel(tail_ref, keep_ref, recv_ref, out_ref):
    tail = pack_sums(read_sums(tail_ref[...]) + read_sums(recv_ref[16 * TOK :, :]))
    for x in range(4):
        for n in range(4):
            m = x * 4 + n
            out_ref[x, n * TOK : (n + 1) * TOK, :] = (
                keep_ref[m].astype(F32) + recv_ref[m * TOK : (m + 1) * TOK, :].astype(F32)
            ).astype(BF16)
        out_ref[x, 4 * TOK :, :] = tail


def route_kernel(
    shard_ref, gain_ref, keep_hbm, place_ref, rank_ref, hits_ref, tail_ref, keep_ref, held_ref, sems
):
    copies = [
        pltpu.make_async_copy(keep_hbm.at[pl.ds(0, 16)], keep_ref, sems.at[0]),
        pltpu.make_async_copy(keep_hbm.at[16, pl.ds(0, TAIL)], tail_ref, sems.at[1]),
    ]
    for copy in copies:
        copy.start()
    held_ref[...] = gain_ref[...]
    dest = shard_ref[...]
    hits = jnp.where(lax.broadcasted_iota(jnp.int32, hits_ref.shape, 0) == dest, 1.0, 0.0)
    hits_ref[...] = hits.astype(BF16)
    earlier = jnp.where(
        lax.broadcasted_iota(jnp.int32, (TOK, TOK), 0)
        < lax.broadcasted_iota(jnp.int32, (TOK, TOK), 1),
        1.0,
        0.0,
    ).astype(BF16)
    counts = jnp.dot(hits.astype(BF16), earlier, preferred_element_type=F32)
    rank = jnp.sum(counts * hits, axis=0, keepdims=True).astype(jnp.int32)
    rank_ref[...] = jnp.broadcast_to(rank, rank_ref.shape)
    row = lax.broadcasted_iota(jnp.int32, (place_ref.shape[0], TOK), 0)
    for j in range(2):
        wanted = dest * PAD + 2 * rank + j
        place_ref[:, j * TOK : (j + 1) * TOK] = jnp.where(row == wanted, 1.0, 0.0).astype(BF16)
    for copy in copies:
        copy.wait()


def pack_kernel(recv_ref, place_ref, rank_ref, hits_ref, out_ref, wide):
    tail = slice(4 * TOK, 4 * TOK + TAIL)

    def total(n):
        part = [recv_ref[x, n * TOK : (n + 1) * TOK, :].astype(F32) for x in range(4)]
        return ((part[0] + part[1]) + (part[2] + part[3])).astype(BF16)

    sums = sum(read_sums(recv_ref[x, tail, :]) for x in range(4))
    sums = jnp.concatenate([sums[0:1], sums[1:2]], axis=1)
    high = sums.astype(BF16).astype(F32)
    slot = lax.broadcasted_iota(jnp.int32, (TILE, TOK), 0) == rank_ref[0:1, :]
    rows = place_ref.shape[0]
    parts = jnp.concatenate(
        [jnp.concatenate([total(z * 2 + j) for z in range(2)], axis=1) for j in range(2)], axis=0
    )
    moved = jnp.dot(place_ref[...], parts, preferred_element_type=F32)
    for z in range(2):
        wide[z * rows : (z + 1) * rows, :] = moved[:, z * TILE : (z + 1) * TILE]
    for n, values in enumerate((high, sums - high)):
        held = jnp.where(slot, values, 0.0).astype(BF16)
        shown = lax.dot_general(
            hits_ref[...], held, (((1,), (1,)), ((), ())), preferred_element_type=F32
        )
        for z in range(2):
            wide[pl.ds(z * rows + 2 * CAP + n, shown.shape[0], stride=PAD), :] = shown
    out_ref[...] = wide[: 2 * rows, :].astype(BF16)


def student_work(rows_hbm, gain, weight_hbm, out_ref, stash_hbm, rows, weight, turned, sems):
    steps = 8
    step = DS // steps
    count = rows.shape[0]
    halves = [pl.ds(0, count // 2), pl.ds(count // 2, count // 2)]
    loads = [
        pltpu.make_async_copy(rows_hbm.at[part], rows.at[part], sems.at[steps + n])
        for n, part in enumerate(halves)
    ]
    loads.append(pltpu.make_async_copy(weight_hbm, weight, sems.at[steps + 2]))
    loads[0].start()
    loads[1].start()
    scale = []
    for part, copy in zip(halves, loads):
        copy.wait()
        if not scale:
            loads[2].start()
        squares = jnp.zeros((count // 2, TILE), F32)
        for n in range(DS // TILE):
            wide = rows[part, n * TILE : (n + 1) * TILE].astype(F32)
            squares = squares + wide * wide
        scale.append(lax.rsqrt(jnp.sum(squares, axis=1, keepdims=True) / DS + EPS))
    scale = jnp.concatenate(scale, axis=0)
    out_ref[...] = jnp.zeros_like(out_ref)
    loads[2].wait()
    copies = []
    for n in range(steps):
        part = slice(n * step, (n + 1) * step)
        normed = (rows[:, part].astype(F32) * scale * gain[:, part]).astype(BF16)
        out_ref[...] += jnp.dot(normed, weight[part, :], preferred_element_type=F32)
        turned[part, :] = jnp.transpose(normed)
        here = pl.ds(n * step, step)
        copies.append(pltpu.make_async_copy(turned.at[here], stash_hbm.at[here], sems.at[n]))
        copies[n].start()
    for copy in copies:
        copy.wait()


def early_student_kernel(
    rows_hbm, gain_ref, weight_hbm, line_ref, out_ref, stash_hbm, head_ref, rows, weight, turned, sems
):
    @pl.when(lax.axis_index("role") == 0)
    def _():
        student_work(
            rows_hbm, gain_ref, weight_hbm, out_ref, stash_hbm, rows, weight, turned, sems
        )
        head_ref[...] = turned[: head_ref.shape[0], :]


def late_student_kernel(
    rows_hbm, gain_ref, weight_hbm, recv_ref, early_hbm, out_ref, stash_hbm, *scratch
):
    @pl.when(lax.axis_index("role") == 1)
    def _():
        student_work(rows_hbm, gain_ref, weight_hbm, out_ref, stash_hbm, *scratch)


def grad_kernel(
    recv_ref, early_ref, late_ref, head_ref, stash_hbm, grad_hbm, wide, turned, grad, sems
):
    steps = sems.shape[1]
    block = DS // steps
    here = [pl.ds(n * block, block) for n in range(steps)]
    loads = {
        n: pltpu.make_async_copy(
            stash_hbm.at[pl.ds(n * block, size * block)],
            turned.at[pl.ds(n * block, size * block)],
            sems.at[0, n],
        )
        for n, size in ((0, 1), (1, 3), (4, 4))
    }
    stores = [
        pltpu.make_async_copy(grad.at[here[n]], grad_hbm.at[here[n]], sems.at[1, n])
        for n in range(steps)
    ]
    early_core = lax.axis_index("role") == 0
    for n, copy in loads.items():
        if n:
            copy.start()

    @pl.when(jnp.logical_not(early_core))
    def _():
        loads[0].start()

    @pl.when(early_core)
    def _():
        turned[:block, :] = head_ref[...]

    half = recv_ref.shape[0] // 2
    count = half // 2
    shards = half // PAD
    row = lax.broadcasted_iota(jnp.int32, (count, 1), 0)
    source = row // (PAD // 2)
    own = lax.broadcasted_iota(jnp.int32, (count, TILE), 1) == row - source * (PAD // 2)
    spread = jnp.where(
        lax.broadcasted_iota(jnp.int32, (count, shards), 1) == source, 1.0, 0.0
    ).astype(BF16)
    row = lax.broadcasted_iota(jnp.int32, (1, count), 1)
    source = row // (PAD // 2)
    row = jnp.where(row - source * (PAD // 2) < CAP, row - source, -1)
    pick = jnp.where(
        lax.broadcasted_iota(jnp.int32, (early_ref.shape[0], count), 0) == row, 1.0, 0.0
    ).astype(BF16)
    wide[: 2 * half, :] = recv_ref[...].astype(F32)

    def every(start, size, stride):
        return sum(wide[pl.ds(z * half + start, size, stride=stride), :] for z in range(2))

    sums = every(2 * CAP, shards, PAD) + every(2 * CAP + 1, shards, PAD)
    inv = lax.rsqrt(sums + EPS)
    high = inv.astype(BF16)
    low = (inv - high.astype(F32)).astype(BF16)
    rows = jnp.dot(
        spread, jnp.concatenate([high, low], axis=1), preferred_element_type=F32
    )
    scale = jnp.sum(
        jnp.where(own, rows[:, :TILE] + rows[:, TILE:], 0.0), axis=1, keepdims=True
    )
    targets = jnp.concatenate(
        [(scale * every(j, count, 2)).astype(BF16) for j in range(2)], axis=1
    )
    wanted = jnp.dot(pick, targets, preferred_element_type=F32)
    student_out = jnp.where(early_core, early_ref[...], late_ref[...])
    delta = ((student_out - wanted) * (1.0 / math.sqrt(TOK))).astype(BF16)

    @pl.when(jnp.logical_not(early_core))
    def _():
        loads[0].wait()

    for n in range(steps):
        if n and n in loads:
            loads[n].wait()
        grad[here[n], :] = jnp.dot(
            turned[here[n], :], delta, preferred_element_type=F32
        ).astype(BF16)
        stores[n].start()
    for copy in stores:
        copy.wait()


def on_device(
    teacher_rows,
    teacher_gain,
    block_index,
    block_tiles,
    student_shard,
    student_rows,
    student_gain,
    student_weight,
):
    shards = lax.axis_size("grp")
    count = student_rows.shape[0]
    send, keep = pl.pallas_call(
        teacher_kernel,
        out_shape=(
            jax.ShapeDtypeStruct((16 * TOK + TAIL, TILE), BF16),
            jax.ShapeDtypeStruct((STASH, TOK, TILE), BF16),
        ),
        in_specs=[HBM] * 4,
        out_specs=(HBM, HBM),
        scratch_shapes=[
            pltpu.SMEM((8, TILE), jnp.int32),
            pltpu.VMEM(teacher_rows.shape, BF16),
            pltpu.VMEM((1, teacher_rows.shape[1]), F32),
            pltpu.VMEM(block_tiles.shape, BF16),
            pltpu.VMEM((32, TOK, TILE), F32),
            pltpu.VMEM((16 * TOK + TAIL, TILE), BF16),
            pltpu.VMEM((16, TOK, TILE), BF16),
            pltpu.VMEM((TAIL, TILE), BF16),
            pltpu.SemaphoreType.DMA((17,)),
        ],
        compiler_params=params(TEACHER_MIB),
        cost_estimate=pl.CostEstimate(flops=540000000, bytes_accessed=6000000, transcendentals=0),
        name="teacher",
    )(block_index.T, teacher_rows, teacher_gain[None, :], block_tiles)
    recv = lax.ppermute(send, "role", [(0, 1), (1, 0)])
    student_shard, student_gain, keep = lax.optimization_barrier(
        (student_shard, student_gain, keep)
    )
    place, rank, hits, tail, keep, gain = pl.pallas_call(
        route_kernel,
        out_shape=(
            jax.ShapeDtypeStruct((shards * PAD, 2 * TOK), BF16),
            jax.ShapeDtypeStruct((8, TOK), jnp.int32),
            jax.ShapeDtypeStruct((shards, TOK), BF16),
            jax.ShapeDtypeStruct((TAIL, TILE), BF16),
            jax.ShapeDtypeStruct((16, TOK, TILE), BF16),
            jax.ShapeDtypeStruct((1, DS), F32),
        ),
        in_specs=[VMEM, VMEM, HBM],
        out_specs=(VMEM,) * 6,
        scratch_shapes=[pltpu.SemaphoreType.DMA((2,))],
        compiler_params=params(ROUTE_MIB),
        cost_estimate=pl.CostEstimate(flops=100000000, bytes_accessed=4000000, transcendentals=0),
        name="route",
    )(student_shard.reshape(1, TOK), student_gain[None, :], keep)
    place, rank, hits, tail, keep, gain, recv = lax.optimization_barrier(
        (place, rank, hits, tail, keep, gain, recv)
    )
    line = pl.pallas_call(
        chip_kernel,
        out_shape=jax.ShapeDtypeStruct((4, 4 * TOK + TAIL, TILE), BF16),
        in_specs=[VMEM] * 3,
        out_specs=VMEM,
        compiler_params=params(),
        cost_estimate=pl.CostEstimate(flops=1000000, bytes_accessed=4000000, transcendentals=0),
        name="chip",
    )(tail, keep, recv)
    student_inputs = (student_rows, gain, student_weight)
    student_shapes = (
        jax.ShapeDtypeStruct((count, 2 * TILE), F32),
        jax.ShapeDtypeStruct((4 * DS, count), BF16),
    )
    student_scratch = [
        pltpu.VMEM(student_rows.shape, BF16),
        pltpu.VMEM(student_weight.shape, BF16),
        pltpu.VMEM((DS, count), BF16),
        pltpu.SemaphoreType.DMA((11,)),
    ]
    early, stash, head = pl.pallas_call(
        early_student_kernel,
        out_shape=(*student_shapes, jax.ShapeDtypeStruct((DS // 8, count), BF16)),
        in_specs=[HBM, VMEM, HBM, VMEM],
        out_specs=(VMEM, HBM, VMEM),
        scratch_shapes=student_scratch,
        compiler_params=params(51),
        cost_estimate=pl.CostEstimate(flops=2000000000, bytes_accessed=10000000, transcendentals=480),
        name="early_student",
    )(*student_inputs, line)
    early, stash, head, line = lax.optimization_barrier((early, stash, head, line))
    groups = [[z * 4 + x for x in range(4)] for z in range(2)]
    line = lax.all_to_all(line, "tp", 0, 0, tiled=True, axis_index_groups=groups)
    packed = pl.pallas_call(
        pack_kernel,
        out_shape=jax.ShapeDtypeStruct((2 * shards * PAD, TILE), BF16),
        in_specs=[VMEM] * 4,
        out_specs=VMEM,
        scratch_shapes=[pltpu.VMEM((2 * shards * PAD + 2 * TAIL, TILE), F32)],
        compiler_params=params(),
        cost_estimate=pl.CostEstimate(flops=400000000, bytes_accessed=2000000, transcendentals=0),
        name="pack",
    )(line, place, rank, hits)
    groups = [
        [(g * 8 + z * 4 + x) * 2 + c for z in range(2) for g in range(shards)]
        for x in range(4)
        for c in range(2)
    ]
    arrived = lax.all_to_all(
        packed.reshape(2 * shards, PAD // 2, 2, TILE),
        ("grp", "tp", "role"),
        split_axis=0,
        concat_axis=0,
        tiled=True,
        axis_index_groups=groups,
    )
    rows = shards * PAD
    arrived = arrived.reshape(2 * rows, TILE)
    late, stash = pl.pallas_call(
        late_student_kernel,
        out_shape=student_shapes,
        in_specs=[HBM, VMEM, HBM, VMEM, HBM],
        out_specs=(VMEM, HBM),
        input_output_aliases={4: 1},
        scratch_shapes=student_scratch,
        compiler_params=params(51),
        cost_estimate=pl.CostEstimate(flops=2000000000, bytes_accessed=10000000, transcendentals=480),
        name="late_student",
    )(*student_inputs, arrived, stash)
    return pl.pallas_call(
        grad_kernel,
        out_shape=jax.ShapeDtypeStruct((DS, 2 * TILE), BF16),
        in_specs=[VMEM] * 4 + [HBM],
        out_specs=HBM,
        scratch_shapes=[
            pltpu.VMEM((2 * rows + 2 * TAIL, TILE), F32),
            pltpu.VMEM((DS, count), BF16),
            pltpu.VMEM((DS, 2 * TILE), BF16),
            pltpu.SemaphoreType.DMA((2, 8)),
        ],
        compiler_params=params(51),
        cost_estimate=pl.CostEstimate(flops=1000000000, bytes_accessed=7000000, transcendentals=0),
        name="grad",
    )(arrived, early, late, head, stash)


def solution(mesh):
    placed = (
        P("grp", ("tp", "role")),
        P(("tp", "role")),
        P(),
        P(("tp", "role"), None, None, None),
        P("grp", None),
        P("grp", None),
        P(),
        P(None, ("tp", "role")),
    )
    return jax.shard_map(
        on_device, mesh=mesh, in_specs=placed, out_specs=P("grp", ("tp", "role")), check_vma=False
    )
```
